32 devices in a mesh: groups: 2 (over x), leaf: 16 (over z, y, core).
Axes of the slice: x: 2, y: 2, z: 4, core: 2. Of those that a mesh axis runs over, the one named last changes fastest.
Arguments:
- vectors: float32 [256, 32, 128], P(('groups', 'leaf')), parts along dimension 0, may hold values from -6 to 6
- near_index: int32 [256, 6], P(('groups', 'leaf')), parts along dimension 0, may hold values from 0 to 127, as said below
- near_block: float32 [256, 6, 128, 128], P(('groups', 'leaf')), parts along dimension 0, may hold values from -0.21875 to 0.21875
- basis: float32 [256, 128, 64], P(('groups', 'leaf')), parts along dimension 0, may hold values from -0.5 to 0.5
- far_index: int32 [256, 8], P(('groups', 'leaf')), parts along dimension 0, may hold values from 0 to 127, as said below
- far_coupling: float32 [256, 8, 64, 64], P(('groups', 'leaf')), parts along dimension 0, may hold values from -0.25 to 0.25
- transfer: float32 [256, 64, 64], P(('groups', 'leaf')), parts along dimension 0, may hold values from -0.25 to 0.25
- up_index: int32 [32, 8], P(('groups', 'leaf')), parts along dimension 0, may hold values from 0 to 15, as said below
- up_coupling: float32 [32, 8, 64, 64], P(('groups', 'leaf')), parts along dimension 0, may hold values from -0.25 to 0.25
Outputs:
- product: float32 [256, 32, 128], P(('groups', 'leaf')), parts along dimension 0
The draws below stay inside these ranges and needn't reach their ends.
There are 2 independent parts, one for each index of `groups`. The reference program is written for one: setup_inputs(seed, part) draws one part's arguments, and reference() takes and returns one part's arrays. A program takes and returns all parts, laid end to end along the dimension named above; each array names one. Nothing has to cross between parts.
Inputs may be any that keep to these rules, and one draw needn't show every extreme that they name: near_index[l, 0] = l, and every leaf's list differs from l by at most 8; slot 1 differs by exactly 8. `far_index`: slot 2 of leaf l is (l + 64) mod 128; every other entry differs from l by 8 + 1 to 24; slot 0 by exactly 24, slot 1 by exactly 9. `up_index`: slot 2 of parent q is (q + 8) mod 16; every other entry differs from q by 1 + 1 to 3; slot 0 by exactly 3, slot 1 by exactly 2.
All inputs are finite; a program needn't handle non-finite values.
Results may differ from the reference program's by a relative error of at most 0.000057.
Values sent between devices are 32-bit elements; how exact they have to be, the bound alone decides.
No kernel may reach another device: no remote copies, remote signals or barrier semaphores. Data moves between devices by JAX's collectives and lax.ppermute only.
A program may use at most 64 MiB of HBM per device.

```python
import jax
import jax.numpy as jnp
from jax import lax

P_SIZE = 128
K = 64
V = 32
NEAR = 6
FAR = 8
FAR_UP = 8
CHILD = 8
LEAF_DEV = 8
LEAVES = 128
PARENTS = 16


def draw_near_index(key, part):
    key = jax.random.fold_in(key, 11)
    leaves = jnp.arange(LEAVES, dtype=jnp.int32)[:, None]
    offsets = jax.random.randint(key, (LEAVES, NEAR), -LEAF_DEV, LEAF_DEV + 1).astype(jnp.int32)
    offsets = offsets.at[:, 0].set(0)
    offsets = offsets.at[:, 1].set(LEAF_DEV)
    target = leaves + offsets
    target = jnp.where((target < 0) | (target >= LEAVES), leaves - offsets, target)
    return target.astype(jnp.int32)


def band_list(key, count, slots, span):
    key_dist, key_sign = jax.random.split(key)
    nodes = jnp.arange(count, dtype=jnp.int32)[:, None]
    distance = jax.random.randint(key_dist, (count, slots), span + 1, 3 * span + 1).astype(jnp.int32)
    distance = distance.at[:, 0].set(3 * span)
    distance = distance.at[:, 1].set(span + 1)
    signs = (jax.random.randint(key_sign, (count, slots), 0, 2) * 2 - 1).astype(jnp.int32)
    target = nodes + signs * distance
    target = jnp.where((target < 0) | (target >= count), nodes - signs * distance, target)
    partner = (nodes[:, 0] + count // 2) % count
    target = target.at[:, 2].set(partner)
    return target.astype(jnp.int32)


def draw_far_index(key, part):
    key = jax.random.fold_in(key, 23)
    return band_list(key, LEAVES, FAR, LEAF_DEV)


def draw_up_index(key, part):
    key = jax.random.fold_in(key, 37)
    return band_list(key, PARENTS, FAR_UP, LEAF_DEV // CHILD)


def steps_of(stream_key, extent, cuts, smallest, top_value):
    def one(dim, parts):
        heights = jax.random.uniform(jax.random.fold_in(jax.random.fold_in(stream_key, 6), dim), (parts,), jnp.float32, smallest / len(cuts), top_value / len(cuts))
        return jnp.repeat(jnp.exp(heights), extent[dim] // parts).reshape((-1,) + (1,) * (len(extent) - dim - 1))

    level = one(*cuts[0])
    for cut in cuts[1:]:
        level = level * one(*cut)
    return level


def scatter_about(own_key, dims, scale, most, cuts=(), held_as=jnp.bfloat16):
    result = scale * jax.random.normal(own_key, dims, jnp.float32)
    if cuts:
        result = result * steps_of(own_key, dims, cuts, -0.22, 0.18)
    return jnp.clip(result, -most, most).astype(held_as)


def setup_inputs(seed: int = 0, part: int = 0) -> dict:
    splits = jax.random.split(jax.random.key(seed), 10)
    part_keys = jax.random.split(jax.random.fold_in(splits[9], part), 10)
    vectors = scatter_about(part_keys[0], (LEAVES, V, P_SIZE), 1.0, 6.0, ((0, 16),), jnp.float32)
    near_index = draw_near_index(jax.random.fold_in(jax.random.fold_in(splits[9], part), 71), part)
    near_block = scatter_about(part_keys[2], (LEAVES, NEAR, P_SIZE, P_SIZE), (P_SIZE * NEAR) ** -0.5, 0.21875, ((0, 16),), jnp.float32)
    basis = scatter_about(part_keys[3], (LEAVES, P_SIZE, K), P_SIZE ** -0.5, 0.5, ((0, 16),), jnp.float32)
    far_index = draw_far_index(jax.random.fold_in(jax.random.fold_in(splits[9], part), 71), part)
    far_coupling = scatter_about(part_keys[5], (LEAVES, FAR, K, K), (K * FAR) ** -0.5, 0.25, ((0, 16),), jnp.float32)
    transfer = scatter_about(part_keys[6], (LEAVES, K, K), (K * CHILD) ** -0.5, 0.25, ((0, 16),), jnp.float32)
    up_index = draw_up_index(jax.random.fold_in(jax.random.fold_in(splits[9], part), 71), part)
    up_coupling = scatter_about(part_keys[8], (PARENTS, FAR_UP, K, K), (K * FAR_UP) ** -0.5, 0.25, ((0, 16),), jnp.float32)
    return dict(vectors=vectors, near_index=near_index, near_block=near_block, basis=basis, far_index=far_index, far_coupling=far_coupling, transfer=transfer, up_index=up_index, up_coupling=up_coupling)


highest = lax.Precision.HIGHEST


def reference(vectors, near_index, near_block, basis, far_index, far_coupling, transfer, up_index, up_coupling):
    leaf_coeffs = jnp.einsum("lvp,lpk->lvk", vectors, basis, precision=highest)
    parents_count = leaf_coeffs.shape[0] // CHILD
    child_coeffs = leaf_coeffs.reshape(parents_count, CHILD, V, K)
    child_transfer = transfer.reshape(parents_count, CHILD, K, K)
    parent_coeffs = jnp.einsum("pcvk,pckm->pvm", child_coeffs, child_transfer, precision=highest)
    parent_far = jnp.einsum("psvk,pskm->pvm", parent_coeffs[up_index], up_coupling, precision=highest)
    downward = jnp.einsum("pvm,pckm->pcvk", parent_far, child_transfer, precision=highest).reshape(leaf_coeffs.shape)
    leaf_far = jnp.einsum("lsvk,lskm->lvm", leaf_coeffs[far_index], far_coupling, precision=highest) + downward
    near_field = jnp.einsum("lsvq,lspq->lvp", vectors[near_index], near_block, precision=highest)
    return near_field + jnp.einsum("lvk,lpk->lvp", leaf_far, basis, precision=highest)
```

```python
import functools

import jax
import jax.numpy as jnp
from jax import lax
from jax.experimental import pallas as pl
from jax.experimental.pallas import tpu as pltpu
from jax.sharding import PartitionSpec as P

REACH = 3
F32 = jnp.float32
NN = (((1,), (0,)), ((), ()))
NT = (((1,), (1,)), ((), ()))
VMEM = pl.BlockSpec(memory_space=pltpu.VMEM)
SMEM = pl.BlockSpec(memory_space=pltpu.SMEM)


def split(x):
    high = x.astype(jnp.bfloat16)
    return high, (x - high.astype(F32)).astype(jnp.bfloat16)


def dot(x, y, dims):
    xh, xl = split(x)
    yh, yl = split(y)
    mul = functools.partial(lax.dot_general, dimension_numbers=dims, preferred_element_type=F32)
    return mul(xh, yh) + (mul(xl, yh) + mul(xh, yl))


def pack(x):
    half = x.shape[0] // 2
    return jnp.concatenate([x[:half], x[half:]], axis=1)


def coeffs_kernel(vectors, basis, transfer, sent, coeffs):
    leaves, rows, points = vectors.shape
    rank = basis.shape[2]
    half = rows // 2
    base = leaves * rows
    parts = []
    for l in range(leaves):
        own = vectors[l]
        sent[l * rows : (l + 1) * rows] = own
        parts.append(dot(own, basis[l], NN))
    whole = jnp.concatenate(parts, axis=1)
    parts.append(dot(whole, transfer[...].reshape(leaves * rank, rank), NN))
    for i, part in enumerate(parts):
        packed = pack(part)
        coeffs[i * half : (i + 1) * half] = packed
        sent[base + i * half : base + (i + 1) * half] = packed


def place(index, here, side):
    away = (index - here) * side
    return jnp.where(jnp.abs(away) <= REACH, away + REACH, 2 * REACH + 1)


def near_kernel(near_index, vectors, near_block, beside, across, near, held):
    leaves, slots = near_index.shape
    rows = vectors.shape[1]
    here = lax.axis_index("leaf")
    side = 1 - 2 * lax.rem(here, 2)
    for l in range(leaves):
        held[l] = across[l * rows : (l + 1) * rows]
        held[leaves + l] = vectors[l]
        held[2 * leaves + l] = beside[l * rows : (l + 1) * rows]
    for l in range(leaves):
        chosen = []
        for s in range(slots):
            index = near_index[l, s]
            device = lax.div(index, leaves)
            away = (device - here) * side
            chosen.append(held[(away + 1) * leaves + (index - device * leaves)])
        inputs = jnp.concatenate(chosen, axis=1)
        blocks = jnp.concatenate([near_block[l, s] for s in range(slots)], axis=1)
        near[l] = dot(inputs, blocks, NT)


def far_kernel(
    far_index, up_index, near, own, beside, across, second, third, opposite, second_beside, third_beside,
    far_coupling, up_coupling, transfer, basis, product, held,
):
    leaves, rows, points = near.shape
    rank = basis.shape[2]
    half = rows // 2
    slots = far_index.shape[1]
    here = lax.axis_index("leaf")
    side = 1 - 2 * lax.rem(here, 2)
    left = lax.broadcasted_iota(jnp.int32, (half, 2 * rank), 1) < rank
    left_all = lax.broadcasted_iota(jnp.int32, (rows, 2 * rank), 1) < rank
    base = leaves * rows
    sources = (third, second, across, own, beside, second_beside, third_beside, opposite)
    for k, source in enumerate(sources):
        skip = source.shape[0] - (leaves + 1) * half
        for i in range(leaves + 1):
            x = source[skip + i * half : skip + (i + 1) * half]
            turned = pltpu.roll(x, rank, 1)
            held[k * (leaves + 1) + i, :half] = jnp.where(left, x, turned)
            held[k * (leaves + 1) + i, half:] = jnp.where(left, turned, x)

    def chosen(u, s):
        if u < leaves:
            index = far_index[u, s]
            device = lax.div(index, leaves)
            return held[place(device, here, side) * (leaves + 1) + (index - device * leaves)]
        return held[place(up_index[0, s], here, side) * (leaves + 1) + leaves]

    def far(u, coupling):
        inputs = [jnp.where(left_all, chosen(u, s), chosen(u, s + 1)) for s in range(0, slots, 2)]
        return dot(jnp.concatenate(inputs, axis=1), coupling.reshape(slots * rank, rank), NN)

    parent_far = far(leaves, up_coupling[0])
    down = dot(parent_far, transfer[...].reshape(leaves * rank, rank), NT)
    for l in range(leaves):
        leaf_far = far(l, far_coupling[l]) + down[:, l * rank : (l + 1) * rank]
        product[l] = near[l] + dot(leaf_far, basis[l], NT)


def routes(groups, count):
    last = count - 1

    def mirrored(step):
        wanted = [(i - step, i) if i % 2 == 0 else (i + step, i) for i in range(count)]
        return [(j, i) for j, i in wanted if 0 <= j <= last]

    def everywhere(pairs):
        return [(g * count + j, g * count + i) for g in range(groups) for j, i in pairs]

    beside = everywhere([(i, i ^ 1) for i in range(count)])
    across = everywhere(mirrored(1))
    if groups > 1:
        across += [(g * count + i, (g + 1) % groups * count + i) for g in range(groups) for i in (0, last)]
    second = everywhere(mirrored(2) + [(1, 0), (last - 1, last)])
    third = everywhere(mirrored(3) + [(0, 2), (2, 0), (last, last - 2), (last - 2, last)])
    opposite = everywhere([(i, (i + count // 2) % count) for i in range(count)])
    return beside, across, second, third, opposite


def per_device(
    groups, vectors, near_index, near_block, basis, far_index, far_coupling, transfer, up_index, up_coupling
):
    leaves, rows, points = vectors.shape
    rank = basis.shape[2]
    packed = (leaves + 1) * rows // 2
    beside_to, across_to, second_to, third_to, opposite_to = routes(groups, lax.axis_size("leaf"))

    def send(x, to):
        return lax.ppermute(x, ("groups", "leaf"), to)

    sent, own = pl.pallas_call(
        coeffs_kernel,
        out_shape=(
            jax.ShapeDtypeStruct((leaves * rows + packed, points), F32),
            jax.ShapeDtypeStruct((packed, points), F32),
        ),
        in_specs=[VMEM] * 3,
        out_specs=(VMEM, VMEM),
    )(vectors, basis, transfer)
    across = send(sent, across_to)
    beside = send(sent, beside_to)
    opposite = send(own, opposite_to)
    third = send(own, third_to)
    second = send(own, second_to)
    second_beside = send(across, beside_to)
    third_beside = send(second, beside_to)
    near = pl.pallas_call(
        near_kernel,
        out_shape=jax.ShapeDtypeStruct(vectors.shape, F32),
        in_specs=[SMEM] + [VMEM] * 4,
        out_specs=VMEM,
        scratch_shapes=[pltpu.VMEM((3 * leaves, rows, points), F32)],
    )(near_index, vectors, near_block, beside, across)
    return pl.pallas_call(
        far_kernel,
        out_shape=jax.ShapeDtypeStruct(vectors.shape, F32),
        in_specs=[SMEM] * 2 + [VMEM] * 13,
        out_specs=VMEM,
        scratch_shapes=[pltpu.VMEM(((2 * REACH + 2) * (leaves + 1), rows, points), F32)],
    )(
        far_index, up_index, near, own, beside, across, second, third, opposite, second_beside, third_beside,
        far_coupling, up_coupling, transfer, basis,
    )


def solution(mesh):
    placed = (
        P(("groups", "leaf"), None, None),
        P(("groups", "leaf"), None),
        P(("groups", "leaf"), None, None, None),
        P(("groups", "leaf"), None, None),
        P(("groups", "leaf"), None),
        P(("groups", "leaf"), None, None, None),
        P(("groups", "leaf"), None, None),
        P(("groups", "leaf"), None),
        P(("groups", "leaf"), None, None, None),
    )
    return jax.shard_map(
        functools.partial(per_device, mesh.shape["groups"]),
        mesh=mesh,
        in_specs=placed,
        out_specs=P(("groups", "leaf"), None, None),
        check_vma=False,
    )
```

```python
import functools

import jax
import jax.numpy as jnp
from jax import lax
from jax.experimental import pallas as pl
from jax.experimental.pallas import tpu as pltpu
from jax.sharding import PartitionSpec as P

REACH = 3
F32 = jnp.float32
NN = (((1,), (0,)), ((), ()))
NT = (((1,), (1,)), ((), ()))
HBM = pl.BlockSpec(memory_space=pltpu.HBM)
VMEM = pl.BlockSpec(memory_space=pltpu.VMEM)
SMEM = pl.BlockSpec(memory_space=pltpu.SMEM)


def cost(us):
    return pl.CostEstimate(flops=us * 500_000_000, bytes_accessed=0, transcendentals=0)


def room(mib):
    return pltpu.CompilerParams(vmem_limit_bytes=mib << 20)


def split(x):
    high = x.astype(jnp.bfloat16)
    return high, (x - high.astype(F32)).astype(jnp.bfloat16)


def dot(x, y, dims):
    xh, xl = split(x)
    yh, yl = split(y)
    mul = functools.partial(lax.dot_general, dimension_numbers=dims, preferred_element_type=F32)
    return mul(xh, yh) + (mul(xl, yh) + mul(xh, yl))


def streamed(blocks, inputs):
    rows = inputs.shape[0]
    bh, bl = split(blocks)
    xh, xl = split(inputs)
    mul = functools.partial(lax.dot_general, dimension_numbers=NT, preferred_element_type=F32)
    both = mul(bh, jnp.concatenate([xh, xl], axis=0))
    return (both[:, :rows] + (both[:, rows:] + mul(bl, xh))).T


def pack(x):
    half = x.shape[0] // 2
    return jnp.concatenate([x[:half], x[half:]], axis=1)


def coeffs_kernel(vectors_in, basis_in, transfer_in, coeffs, vectors, basis, transfer, arrived):
    leaves, rows, points = vectors.shape
    copies = [
        pltpu.make_async_copy(there, here, arrived.at[i])
        for i, (there, here) in enumerate(((vectors_in, vectors), (basis_in, basis), (transfer_in, transfer)))
    ]
    for copy in copies:
        copy.start()
    copies[0].wait()
    copies[1].wait()
    rank = basis.shape[1]
    half = rows // 2
    parts = []
    for l in range(leaves):
        parts.append(dot(vectors[l], basis[l], NT))
    whole = jnp.concatenate(parts, axis=1)
    copies[2].wait()
    parts.append(dot(whole, transfer[...].reshape(leaves * rank, rank), NN))
    for i, part in enumerate(parts):
        coeffs[i * half : (i + 1) * half] = pack(part)


def place(index, here, side):
    away = (index - here) * side
    return jnp.where(jnp.abs(away) <= REACH, away + REACH, 2 * REACH + 1)


def near_kernel(near_index, near_block, own, beside, across, near, held):
    leaves, slots = near_index.shape
    rows = near.shape[1]
    here = lax.axis_index("leaf")
    side = 1 - 2 * lax.rem(here, 2)
    for l in range(leaves):
        held[l] = across[l]
        held[leaves + l] = own[l]
        held[2 * leaves + l] = beside[l]
    for l in range(leaves):
        chosen = []
        for s in range(slots):
            index = near_index[l, s]
            device = lax.div(index, leaves)
            away = (device - here) * side
            chosen.append(held[(away + 1) * leaves + (index - device * leaves)])
        inputs = jnp.concatenate(chosen, axis=1)
        blocks = jnp.concatenate([near_block[l, s] for s in range(slots)], axis=1)
        near[l] = streamed(blocks, inputs)


def far_kernel(
    far_index, up_index, near, own, beside, across, second, third, opposite, second_beside, third_beside,
    far_coupling, up_coupling, transfer, basis, product, held,
):
    leaves, rows, points = near.shape
    rank = basis.shape[1]
    half = rows // 2
    slots = far_index.shape[1]
    here = lax.axis_index("leaf")
    side = 1 - 2 * lax.rem(here, 2)
    left = lax.broadcasted_iota(jnp.int32, (half, 2 * rank), 1) < rank
    left_all = lax.broadcasted_iota(jnp.int32, (rows, 2 * rank), 1) < rank
    base = leaves * rows
    sources = (third, second, across, own, beside, second_beside, third_beside, opposite)
    for k, source in enumerate(sources):
        for i in range(leaves + 1):
            x = source[i * half : (i + 1) * half]
            turned = pltpu.roll(x, rank, 1)
            held[k * (leaves + 1) + i, :half] = jnp.where(left, x, turned)
            held[k * (leaves + 1) + i, half:] = jnp.where(left, turned, x)

    def chosen(u, s):
        if u < leaves:
            index = far_index[u, s]
            device = lax.div(index, leaves)
            return held[place(device, here, side) * (leaves + 1) + (index - device * leaves)]
        return held[place(up_index[0, s], here, side) * (leaves + 1) + leaves]

    def far(u, coupling):
        inputs = [jnp.where(left_all, chosen(u, s), chosen(u, s + 1)) for s in range(0, slots, 2)]
        return dot(jnp.concatenate(inputs, axis=1), coupling.reshape(slots * rank, rank), NN)

    parent_far = far(leaves, up_coupling[0])
    down = dot(parent_far, transfer[...].reshape(leaves * rank, rank), NT)
    leaf_fars = [far(l, far_coupling[l]) for l in range(leaves)]
    for l in range(leaves):
        leaf_far = leaf_fars[l] + down[:, l * rank : (l + 1) * rank]
        product[l] = near[l] + dot(leaf_far, basis[l], NN)


def routes(groups, count):
    last = count - 1

    def mirrored(step):
        wanted = [(i - step, i) if i % 2 == 0 else (i + step, i) for i in range(count)]
        return [(j, i) for j, i in wanted if 0 <= j <= last]

    def everywhere(pairs):
        return [(g * count + j, g * count + i) for g in range(groups) for j, i in pairs]

    beside = everywhere([(i, i ^ 1) for i in range(count)])
    across = everywhere(mirrored(1))
    if groups > 1:
        across += [(g * count + i, (g + 1) % groups * count + i) for g in range(groups) for i in (0, last)]
    second = everywhere(mirrored(2) + [(1, 0), (last - 1, last)])
    third = everywhere(mirrored(3) + [(0, 2), (2, 0), (last, last - 2), (last - 2, last)])
    opposite = everywhere([(i, (i + count // 2) % count) for i in range(count)])
    return beside, across, second, third, opposite


def per_device(
    groups, vectors, near_index, near_block, basis, far_index, far_coupling, transfer, up_index, up_coupling
):
    leaves, rows, points = vectors.shape
    rank = basis.shape[2]
    packed = (leaves + 1) * rows // 2
    basis = jnp.swapaxes(basis, 1, 2)
    beside_to, across_to, second_to, third_to, opposite_to = routes(groups, lax.axis_size("leaf"))

    def send(x, to):
        return lax.ppermute(x, ("groups", "leaf"), to)

    vectors_across = send(vectors, across_to)
    vectors_beside = send(vectors, beside_to)
    own = pl.pallas_call(
        coeffs_kernel,
        out_shape=jax.ShapeDtypeStruct((packed, points), F32),
        in_specs=[HBM] * 3,
        out_specs=VMEM,
        scratch_shapes=[
            pltpu.VMEM(vectors.shape, F32),
            pltpu.VMEM(basis.shape, F32),
            pltpu.VMEM(transfer.shape, F32),
            pltpu.SemaphoreType.DMA((3,)),
        ],
        compiler_params=room(4),
        cost_estimate=cost(5),
    )(*(pltpu.with_memory_space_constraint(x, pltpu.HBM) for x in (vectors, basis, transfer)))
    opposite = send(own, opposite_to)
    across = send(own, across_to)
    second = send(own, second_to)
    third = send(own, third_to)
    beside = send(own, beside_to)
    near = pl.pallas_call(
        near_kernel,
        out_shape=jax.ShapeDtypeStruct(vectors.shape, F32),
        in_specs=[SMEM] + [VMEM] * 4,
        compiler_params=room(8),
        cost_estimate=cost(3),
        out_specs=VMEM,
        scratch_shapes=[pltpu.VMEM((3 * leaves, rows, points), F32)],
    )(near_index, near_block, vectors, vectors_beside, vectors_across)
    across, second, near = lax.optimization_barrier((across, second, near))
    second_beside = send(across, beside_to)
    third_beside = send(second, beside_to)
    return pl.pallas_call(
        far_kernel,
        out_shape=jax.ShapeDtypeStruct(vectors.shape, F32),
        in_specs=[SMEM] * 2 + [VMEM] * 13,
        compiler_params=room(10),
        cost_estimate=cost(3),
        out_specs=VMEM,
        scratch_shapes=[pltpu.VMEM(((2 * REACH + 2) * (leaves + 1), rows, points), F32)],
    )(
        far_index, up_index, near, own, beside, across, second, third, opposite, second_beside, third_beside,
        far_coupling, up_coupling, transfer, basis,
    )


def solution(mesh):
    placed = (
        P(("groups", "leaf"), None, None),
        P(("groups", "leaf"), None),
        P(("groups", "leaf"), None, None, None),
        P(("groups", "leaf"), None, None),
        P(("groups", "leaf"), None),
        P(("groups", "leaf"), None, None, None),
        P(("groups", "leaf"), None, None),
        P(("groups", "leaf"), None),
        P(("groups", "leaf"), None, None, None),
    )
    return jax.shard_map(
        functools.partial(per_device, mesh.shape["groups"]),
        mesh=mesh,
        in_specs=placed,
        out_specs=P(("groups", "leaf"), None, None),
        check_vma=False,
    )
```

```python
import functools

import jax
import jax.numpy as jnp
from jax import lax
from jax.experimental import pallas as pl
from jax.experimental.pallas import tpu as pltpu
from jax.sharding import PartitionSpec as P

REACH = 3
F32 = jnp.float32
NN = (((1,), (0,)), ((), ()))
NT = (((1,), (1,)), ((), ()))
HBM = pl.BlockSpec(memory_space=pltpu.HBM)
VMEM = pl.BlockSpec(memory_space=pltpu.VMEM)


def cost(us):
    return pl.CostEstimate(flops=us * 500_000_000, bytes_accessed=0, transcendentals=0)


def room(mib):
    return pltpu.CompilerParams(vmem_limit_bytes=mib << 20)


def split(x):
    high = x.astype(jnp.bfloat16)
    return high, (x - high.astype(F32)).astype(jnp.bfloat16)


def mul(x, y, dims):
    return lax.dot_general(x, y, dims, preferred_element_type=F32)


def dot(x, y, dims):
    rows = x.shape[0]
    xh, xl = split(x)
    yh, yl = split(y)
    both = mul(jnp.concatenate([xh, xl], axis=0), yh, dims)
    return both[:rows] + (both[rows:] + mul(xh, yl, dims))


def streamed(blocks, inputs):
    rows = inputs.shape[0]
    bh, bl = split(blocks)
    xh, xl = split(inputs)
    both = mul(bh, jnp.concatenate([xh, xl], axis=0), NT)
    return (both[:, :rows] + (both[:, rows:] + mul(bl, xh, NT))).T


def pack(x):
    half = x.shape[0] // 2
    return jnp.concatenate([x[:half], x[half:]], axis=1)


def coeffs_kernel(vectors_in, basis_in, transfer_in, coeffs, vectors, basis, transfer, arrived):
    leaves, rows, points = vectors.shape
    copies = [
        pltpu.make_async_copy(there, here, arrived.at[i])
        for i, (there, here) in enumerate(((vectors_in, vectors), (basis_in, basis), (transfer_in, transfer)))
    ]
    for copy in copies:
        copy.start()
    copies[0].wait()
    copies[1].wait()
    rank = basis.shape[1]
    half = rows // 2
    parts = []
    for l in range(leaves):
        parts.append(dot(vectors[l], basis[l], NT))
    whole = jnp.concatenate(parts, axis=1)
    copies[2].wait()
    parts.append(dot(whole, transfer[...].reshape(leaves * rank, rank), NN))
    for i, part in enumerate(parts):
        coeffs[i * half : (i + 1) * half] = pack(part)


def place(index, here):
    differ = index ^ here
    elsewhere = jnp.where(jnp.abs(index - here) <= REACH, 6, 7)
    return jnp.where(differ < 4, differ, jnp.where((index ^ other_side_of(here)) & -2 == 0, 4 + (differ & 1), elsewhere))


def other_side_of(core):
    return core - 2 + 2 * (core & 2)


def near_kernel(near_index, near_block, own, beside, across, near, held):
    leaves, slots = near_index.shape
    rows = near.shape[1]
    here = lax.axis_index("leaf")
    side = 1 - 2 * lax.rem(here, 2)
    for l in range(leaves):
        held[l] = across[l]
        held[leaves + l] = own[l]
        held[2 * leaves + l] = beside[l]
    index = near_index[...]
    device = lax.div(index, leaves)
    places = ((device - here) * side + 1) * leaves + (index - device * leaves)
    for l in range(leaves):
        chosen = [held[places[l, s]] for s in range(slots)]
        inputs = jnp.concatenate(chosen, axis=1)
        blocks = jnp.concatenate([near_block[l, s] for s in range(slots)], axis=1)
        near[l] = streamed(blocks, inputs)


def far_kernel(
    far_index, up_index, near, own, beside, pair, pair_beside, side, side_beside, third, opposite,
    far_coupling, up_coupling, transfer, basis, product, held,
):
    leaves, rows, points = near.shape
    rank = basis.shape[1]
    half = rows // 2
    slots = far_index.shape[1]
    here = lax.axis_index("leaf")
    left = lax.broadcasted_iota(jnp.int32, (half, 2 * rank), 1) < rank
    left_all = lax.broadcasted_iota(jnp.int32, (rows, 2 * rank), 1) < rank
    base = leaves * rows
    sources = (own, beside, pair, pair_beside, side, side_beside, third, opposite)
    for k, source in enumerate(sources):
        for i in range(leaves + 1):
            x = source[i * half : (i + 1) * half]
            turned = pltpu.roll(x, rank, 1)
            held[k * (leaves + 1) + i, :half] = jnp.where(left, x, turned)
            held[k * (leaves + 1) + i, half:] = jnp.where(left, turned, x)

    index = far_index[...]
    device = lax.div(index, leaves)
    places = place(device, here) * (leaves + 1) + (index - device * leaves)
    up_places = place(up_index[...], here) * (leaves + 1) + leaves

    def chosen(u, s):
        return held[places[u, s] if u < leaves else up_places[0, s]]

    def far(u, coupling):
        inputs = [jnp.where(left_all, chosen(u, s), chosen(u, s + 1)) for s in range(0, slots, 2)]
        return dot(jnp.concatenate(inputs, axis=1), coupling.reshape(slots * rank, rank), NN)

    parent_far = far(leaves, up_coupling[0])
    down = dot(parent_far, transfer[...].reshape(leaves * rank, rank), NT)
    leaf_fars = [far(l, far_coupling[l]) for l in range(leaves)]
    for l in range(leaves):
        leaf_far = leaf_fars[l] + down[:, l * rank : (l + 1) * rank]
        product[l] = near[l] + dot(leaf_far, basis[l], NN)


def other_side(core):
    return core + 2 if core & 2 else core - 2


def routes(groups, count):
    last = count - 1
    ends = (0, 1, last - 1, last)

    def everywhere(pairs):
        return [(g * count + j, g * count + i) for g in range(groups) for j, i in pairs]

    def mirrored(step):
        wanted = [(i - step, i) if i % 2 == 0 else (i + step, i) for i in range(count)]
        return [(j, i) for j, i in wanted if 0 <= j <= last]

    beside = everywhere([(i ^ 1, i) for i in range(count)])
    pair = everywhere([(i ^ 2, i) for i in range(count)])
    opposite = everywhere([((i + count // 2) % count, i) for i in range(count)])
    third = everywhere(mirrored(3) + [(0, 2), (2, 0), (last, last - 2), (last - 2, last)])
    across = everywhere(mirrored(1))
    side = everywhere([(other_side(i), i) for i in range(count) if i not in ends])
    if groups > 1:
        across += [(g * count + i, (g + 1) % groups * count + i) for g in range(groups) for i in (0, last)]
        side += [(g * count + i, (g + 1) % groups * count + i) for g in range(groups) for i in ends]
    return beside, across, pair, side, third, opposite


def per_device(
    groups, vectors, near_index, near_block, basis, far_index, far_coupling, transfer, up_index, up_coupling
):
    leaves, rows, points = vectors.shape
    rank = basis.shape[2]
    packed = (leaves + 1) * rows // 2
    basis = jnp.swapaxes(basis, 1, 2)
    beside_to, across_to, pair_to, side_to, third_to, opposite_to = routes(groups, lax.axis_size("leaf"))

    def send(x, to):
        return lax.ppermute(x, ("groups", "leaf"), to)

    vectors_across = send(vectors, across_to)
    vectors_beside = send(vectors, beside_to)
    own = pl.pallas_call(
        coeffs_kernel,
        out_shape=jax.ShapeDtypeStruct((packed, points), F32),
        in_specs=[HBM] * 3,
        out_specs=VMEM,
        scratch_shapes=[
            pltpu.VMEM(vectors.shape, F32),
            pltpu.VMEM(basis.shape, F32),
            pltpu.VMEM(transfer.shape, F32),
            pltpu.SemaphoreType.DMA((3,)),
        ],
        compiler_params=room(4),
        cost_estimate=cost(5),
    )(*(pltpu.with_memory_space_constraint(x, pltpu.HBM) for x in (vectors, basis, transfer)))
    pair = send(own, pair_to)
    side = send(own, side_to)
    opposite = send(own, opposite_to)
    third = send(own, third_to)
    beside = send(own, beside_to)
    vectors_across, vectors_beside, side, pair = lax.optimization_barrier((vectors_across, vectors_beside, side, pair))
    pair_beside = send(pair, beside_to)
    side_beside = send(side, beside_to)
    near = pl.pallas_call(
        near_kernel,
        out_shape=jax.ShapeDtypeStruct(vectors.shape, F32),
        in_specs=[VMEM] * 5,
        compiler_params=room(8),
        cost_estimate=cost(3),
        out_specs=VMEM,
        scratch_shapes=[pltpu.VMEM((3 * leaves, rows, points), F32)],
    )(near_index, near_block, vectors, vectors_beside, vectors_across)
    return pl.pallas_call(
        far_kernel,
        out_shape=jax.ShapeDtypeStruct(vectors.shape, F32),
        in_specs=[VMEM] * 15,
        compiler_params=room(10),
        cost_estimate=cost(3),
        out_specs=VMEM,
        scratch_shapes=[pltpu.VMEM((8 * (leaves + 1), rows, points), F32)],
    )(
        far_index, up_index, near, own, beside, pair, pair_beside, side, side_beside, third, opposite,
        far_coupling, up_coupling, transfer, basis,
    )


def solution(mesh):
    placed = (
        P(("groups", "leaf"), None, None),
        P(("groups", "leaf"), None),
        P(("groups", "leaf"), None, None, None),
        P(("groups", "leaf"), None, None),
        P(("groups", "leaf"), None),
        P(("groups", "leaf"), None, None, None),
        P(("groups", "leaf"), None, None),
        P(("groups", "leaf"), None),
        P(("groups", "leaf"), None, None, None),
    )
    return jax.shard_map(
        functools.partial(per_device, mesh.shape["groups"]),
        mesh=mesh,
        in_specs=placed,
        out_specs=P(("groups", "leaf"), None, None),
        check_vma=False,
    )
```

```python
import functools

import jax
import jax.numpy as jnp
from jax import lax
from jax.experimental import pallas as pl
from jax.experimental.pallas import tpu as pltpu
from jax.sharding import PartitionSpec as P

PARTNER = 2
F32 = jnp.float32
NN = (((1,), (0,)), ((), ()))
NT = (((1,), (1,)), ((), ()))
HBM = pl.BlockSpec(memory_space=pltpu.HBM)
VMEM = pl.BlockSpec(memory_space=pltpu.VMEM)


def cost(us):
    return pl.CostEstimate(flops=us * 500_000_000, bytes_accessed=0, transcendentals=0)


def room(mib):
    return pltpu.CompilerParams(vmem_limit_bytes=mib << 20)


def split(x):
    high = x.astype(jnp.bfloat16)
    return high, (x - high.astype(F32)).astype(jnp.bfloat16)


def mul(x, y, dims):
    return lax.dot_general(x, y, dims, preferred_element_type=F32)


def dot(x, y, dims):
    rows = x.shape[0]
    xh, xl = split(x)
    yh, yl = split(y)
    both = mul(jnp.concatenate([xh, xl], axis=0), yh, dims)
    return both[:rows] + (both[rows:] + mul(xh, yl, dims))


def streamed(blocks, inputs):
    rows = inputs.shape[0]
    bh, bl = split(blocks)
    xh, xl = split(inputs)
    both = mul(bh, jnp.concatenate([xh, xl], axis=0), NT)
    return (both[:, :rows] + (both[:, rows:] + mul(bl, xh, NT))).T


def pack(x):
    half = x.shape[0] // 2
    return jnp.concatenate([x[:half], x[half:]], axis=1)


def coeffs_kernel(vectors_in, basis_in, transfer_in, coeffs, longer, vectors, basis, transfer, arrived):
    leaves, rows, points = vectors.shape
    copies = [
        pltpu.make_async_copy(there, here, arrived.at[i])
        for i, (there, here) in enumerate(((vectors_in, vectors), (basis_in, basis), (transfer_in, transfer)))
    ]
    for copy in copies:
        copy.start()
    copies[0].wait()
    copies[1].wait()
    rank = basis.shape[1]
    half = rows // 2
    parts = []
    for l in range(leaves):
        parts.append(dot(vectors[l], basis[l], NT))
    whole = jnp.concatenate(parts, axis=1)
    copies[2].wait()
    parts.append(dot(whole, transfer[...].reshape(leaves * rank, rank), NN))
    for i, part in enumerate(parts):
        packed = pack(part)
        coeffs[i * half : (i + 1) * half] = packed
        longer[i * half : (i + 1) * half] = packed
    longer[len(parts) * half :] = jnp.zeros_like(longer[len(parts) * half :])


def place(index, here):
    differ = index ^ here
    side = (index ^ other_side_of(here)) & -2 == 0
    return jnp.where(differ & -4 == 0, differ, jnp.where(side, 4 + (differ & 1), 6))


def other_side_of(core):
    return core - 2 + 2 * (core & 2)


def near_kernel(near_index, near_block, own, beside, across, near, held):
    leaves, slots = near_index.shape
    rows = near.shape[1]
    here = lax.axis_index("leaf")
    side = 1 - 2 * lax.rem(here, 2)
    for l in range(leaves):
        held[l] = across[l]
        held[leaves + l] = own[l]
        held[2 * leaves + l] = beside[l]
    index = near_index[...]
    device = lax.div(index, leaves)
    places = ((device - here) * side + 1) * leaves + (index - device * leaves)
    for l in range(leaves):
        chosen = [held[places[l, s]] for s in range(slots)]
        inputs = jnp.concatenate(chosen, axis=1)
        blocks = jnp.concatenate([near_block[l, s] for s in range(slots)], axis=1)
        near[l] = streamed(blocks, inputs)


def partner_matrices_kernel(far_coupling, up_coupling, transfer, basis, high, low):
    leaves, rank, points = basis.shape
    through = dot(up_coupling[0, PARTNER], transfer[...].reshape(leaves * rank, rank), NT)
    for l in range(leaves):
        two = jnp.concatenate([far_coupling[l, PARTNER], through[:, l * rank : (l + 1) * rank]], axis=0)
        high[l], low[l] = split(dot(two, basis[l], NN))


def doubled(x, left):
    turned = pltpu.roll(x, x.shape[1] // 2, 1)
    return jnp.where(left, x, turned), jnp.where(left, turned, x)


def far_kernel(
    far_index, up_index, near, own, beside, pair, pair_beside, side, side_beside, third,
    far_coupling, up_coupling, transfer, basis, base, held,
):
    leaves, rows, points = near.shape
    rank = basis.shape[1]
    half = rows // 2
    slots = [s for s in range(far_index.shape[1]) if s != PARTNER]
    here = lax.axis_index("leaf")
    left = lax.broadcasted_iota(jnp.int32, (half, 2 * rank), 1) < rank
    left_all = lax.broadcasted_iota(jnp.int32, (rows, 2 * rank), 1) < rank
    sources = (own, beside, pair, pair_beside, side, side_beside, third)
    for k, source in enumerate(sources):
        for i in range(leaves + 1):
            block = k * (leaves + 1) + i
            held[block, :half], held[block, half:] = doubled(source[i * half : (i + 1) * half], left)
    index = far_index[...]
    device = lax.div(index, leaves)
    places = place(device, here) * (leaves + 1) + (index - device * leaves)
    up_places = place(up_index[...], here) * (leaves + 1) + leaves

    def chosen(u, s):
        return held[places[u, s] if u < leaves else up_places[0, s]]

    def far(u, coupling):
        inputs = [jnp.where(left_all, chosen(u, s), chosen(u, t)) for s, t in zip(slots[0:-1:2], slots[1::2])]
        if len(slots) % 2:
            inputs.append(chosen(u, slots[-1])[:, :rank])
        return dot(jnp.concatenate(inputs, axis=1), jnp.concatenate([coupling[s] for s in slots], axis=0), NN)

    parent_far = far(leaves, up_coupling[0])
    down = dot(parent_far, transfer[...].reshape(leaves * rank, rank), NT)
    leaf_fars = [far(l, far_coupling[l]) for l in range(leaves)]
    for l in range(leaves):
        leaf_far = leaf_fars[l] + down[:, l * rank : (l + 1) * rank]
        base[l] = near[l] + dot(leaf_far, basis[l], NN)


def partner_kernel(base, opposite, high, low, product):
    leaves, rows, points = base.shape
    half = rows // 2
    left = lax.broadcasted_iota(jnp.int32, (half, points), 1) < points // 2
    blocks = [doubled(opposite[i * half : (i + 1) * half], left) for i in range(leaves + 1)]
    parent = blocks[leaves]
    for l in range(leaves):
        inputs = jnp.concatenate([jnp.where(left, blocks[l][i], parent[i]) for i in range(2)], axis=0)
        xh, xl = split(inputs)
        both = mul(jnp.concatenate([xh, xl], axis=0), high[l], NN)
        product[l] = base[l] + (both[:rows] + (both[rows:] + mul(xh, low[l], NN)))


def other_side(core):
    return core + 2 if core & 2 else core - 2


def routes(groups, count):
    last = count - 1
    ends = (0, 1, last - 1, last)

    def everywhere(pairs):
        return [(g * count + j, g * count + i) for g in range(groups) for j, i in pairs]

    def mirrored(step):
        wanted = [(i - step, i) if i % 2 == 0 else (i + step, i) for i in range(count)]
        return [(j, i) for j, i in wanted if 0 <= j <= last]

    beside = everywhere([(i ^ 1, i) for i in range(count)])
    pair = everywhere([(i ^ 2, i) for i in range(count)])
    opposite = everywhere([((i + count // 2) % count, i) for i in range(count)])
    third = everywhere(mirrored(3))
    across = everywhere(mirrored(1))
    side = everywhere([(other_side(i), i) for i in range(count) if i not in ends])
    if groups > 1:
        across += [(g * count + i, (g + 1) % groups * count + i) for g in range(groups) for i in (0, last)]
        third += [(g * count + i, (g + 1) % groups * count + i) for g in range(groups) for i in (0, 2, last - 2, last)]
        side += [(g * count + i, (g + 1) % groups * count + i) for g in range(groups) for i in ends]
    return beside, across, pair, side, third, opposite


def per_device(
    groups, vectors, near_index, near_block, basis, far_index, far_coupling, transfer, up_index, up_coupling
):
    leaves, rows, points = vectors.shape
    rank = basis.shape[2]
    packed = (leaves + 1) * rows // 2
    basis = jnp.swapaxes(basis, 1, 2)
    beside_to, across_to, pair_to, side_to, third_to, opposite_to = routes(groups, lax.axis_size("leaf"))

    def send(x, to):
        return lax.ppermute(x, ("groups", "leaf"), to)

    vectors_across = send(vectors, across_to)
    vectors_beside = send(vectors, beside_to)
    own, own_longer = pl.pallas_call(
        coeffs_kernel,
        out_shape=tuple(jax.ShapeDtypeStruct((packed + extra, points), F32) for extra in (0, 8)),
        in_specs=[HBM] * 3,
        out_specs=(VMEM, VMEM),
        scratch_shapes=[
            pltpu.VMEM(vectors.shape, F32),
            pltpu.VMEM(basis.shape, F32),
            pltpu.VMEM(transfer.shape, F32),
            pltpu.SemaphoreType.DMA((3,)),
        ],
        compiler_params=room(4),
        cost_estimate=cost(5),
    )(*(pltpu.with_memory_space_constraint(x, pltpu.HBM) for x in (vectors, basis, transfer)))
    own, vectors_beside = lax.optimization_barrier((own, vectors_beside))
    pair = send(own, pair_to)
    side = send(own, side_to)
    opposite = send(own_longer, opposite_to)
    third = send(own, third_to)
    beside = send(own, beside_to)
    whole = jax.ShapeDtypeStruct(vectors.shape, F32)
    parts = jax.ShapeDtypeStruct((leaves, 2 * rank, points), jnp.bfloat16)
    near = pl.pallas_call(
        near_kernel,
        out_shape=whole,
        in_specs=[VMEM] * 5,
        out_specs=VMEM,
        scratch_shapes=[pltpu.VMEM((3 * leaves, rows, points), F32)],
        compiler_params=room(8),
        cost_estimate=cost(0),
    )(near_index, near_block, vectors, vectors_beside, vectors_across)
    near, side, pair = lax.optimization_barrier((near, side, pair))
    pair_beside = send(pair, beside_to)
    side_beside = send(side, beside_to)
    high, low = pl.pallas_call(
        partner_matrices_kernel,
        out_shape=(parts, parts),
        in_specs=[VMEM] * 4,
        out_specs=(VMEM, VMEM),
        compiler_params=room(4),
        cost_estimate=cost(3),
    )(far_coupling, up_coupling, transfer, basis)
    base = pl.pallas_call(
        far_kernel,
        out_shape=whole,
        in_specs=[VMEM] * 14,
        out_specs=VMEM,
        scratch_shapes=[pltpu.VMEM((7 * (leaves + 1), rows, points), F32)],
        compiler_params=room(10),
        cost_estimate=cost(0),
    )(
        far_index, up_index, near, own, beside, pair, pair_beside, side, side_beside, third,
        far_coupling, up_coupling, transfer, basis,
    )
    return pl.pallas_call(
        partner_kernel,
        out_shape=whole,
        in_specs=[VMEM] * 4,
        out_specs=VMEM,
        compiler_params=room(4),
        cost_estimate=cost(0),
    )(base, opposite, high, low)


def solution(mesh):
    placed = (
        P(("groups", "leaf"), None, None),
        P(("groups", "leaf"), None),
        P(("groups", "leaf"), None, None, None),
        P(("groups", "leaf"), None, None),
        P(("groups", "leaf"), None),
        P(("groups", "leaf"), None, None, None),
        P(("groups", "leaf"), None, None),
        P(("groups", "leaf"), None),
        P(("groups", "leaf"), None, None, None),
    )
    return jax.shard_map(
        functools.partial(per_device, mesh.shape["groups"]),
        mesh=mesh,
        in_specs=placed,
        out_specs=P(("groups", "leaf"), None, None),
        check_vma=False,
    )
```

```python
import functools

import jax
import jax.numpy as jnp
from jax import lax
from jax.experimental import pallas as pl
from jax.experimental.pallas import tpu as pltpu
from jax.sharding import PartitionSpec as P

PARTNER = 2
F32 = jnp.float32
NN = (((1,), (0,)), ((), ()))
NT = (((1,), (1,)), ((), ()))
HBM = pl.BlockSpec(memory_space=pltpu.HBM)
VMEM = pl.BlockSpec(memory_space=pltpu.VMEM)


def cost(us):
    return pl.CostEstimate(flops=us * 500_000_000, bytes_accessed=0, transcendentals=0)


def room(mib):
    return pltpu.CompilerParams(vmem_limit_bytes=mib << 20)


def split(x):
    high = x.astype(jnp.bfloat16)
    return high, (x - high.astype(F32)).astype(jnp.bfloat16)


def mul(x, y, dims):
    return lax.dot_general(x, y, dims, preferred_element_type=F32)


def dot(x, y, dims):
    rows = x.shape[0]
    xh, xl = split(x)
    yh, yl = split(y)
    both = mul(jnp.concatenate([xh, xl], axis=0), yh, dims)
    return both[:rows] + (both[rows:] + mul(xh, yl, dims))


def streamed(blocks, inputs):
    rows = inputs.shape[0]
    bh, bl = split(blocks)
    xh, xl = split(inputs)
    both = mul(bh, jnp.concatenate([xh, xl], axis=0), NT)
    return (both[:, :rows] + (both[:, rows:] + mul(bl, xh, NT))).T


def pack(x):
    half = x.shape[0] // 2
    return jnp.concatenate([x[:half], x[half:]], axis=1)


def coeffs_kernel(vectors_in, basis_in, transfer_in, coeffs, longer, vectors, basis, transfer, arrived):
    leaves, rows, points = vectors.shape
    copies = [
        pltpu.make_async_copy(there, here, arrived.at[i])
        for i, (there, here) in enumerate(((vectors_in, vectors), (basis_in, basis), (transfer_in, transfer)))
    ]
    for copy in copies:
        copy.start()
    copies[0].wait()
    copies[1].wait()
    rank = basis.shape[1]
    half = rows // 2
    parts = []
    for l in range(leaves):
        parts.append(dot(vectors[l], basis[l], NT))
    whole = jnp.concatenate(parts, axis=1)
    copies[2].wait()
    parts.append(dot(whole, transfer[...].reshape(leaves * rank, rank), NN))
    for i, part in enumerate(parts):
        packed = pack(part)
        coeffs[i * half : (i + 1) * half] = packed
        longer[i * half : (i + 1) * half] = packed
    longer[len(parts) * half :] = jnp.zeros_like(longer[len(parts) * half :])


def place(index, here):
    differ = index ^ here
    side = (index ^ other_side_of(here)) & -2 == 0
    return jnp.where(differ & -4 == 0, differ, jnp.where(side, 4 + (differ & 1), 6))


def other_side_of(core):
    return core - 2 + 2 * (core & 2)


def near_kernel(near_index, near_block, own, beside, across, near, held):
    leaves, slots = near_index.shape
    rows = near.shape[1]
    here = lax.axis_index("leaf")
    side = 1 - 2 * lax.rem(here, 2)
    for l in range(leaves):
        held[l] = across[l]
        held[leaves + l] = own[l]
        held[2 * leaves + l] = beside[l]
    index = near_index[...]
    device = lax.div(index, leaves)
    places = ((device - here) * side + 1) * leaves + (index - device * leaves)
    for l in range(leaves):
        chosen = [held[places[l, s]] for s in range(slots)]
        inputs = jnp.concatenate(chosen, axis=1)
        blocks = jnp.concatenate([near_block[l, s] for s in range(slots)], axis=1)
        near[l] = streamed(blocks, inputs)


def partner_matrices_kernel(far_coupling, up_coupling, transfer, basis, high, low):
    leaves, rank, points = basis.shape
    through = dot(up_coupling[0, PARTNER], transfer[...].reshape(leaves * rank, rank), NT)
    for l in range(leaves):
        two = jnp.concatenate([far_coupling[l, PARTNER], through[:, l * rank : (l + 1) * rank]], axis=0)
        high[l], low[l] = split(dot(two, basis[l], NN))


def doubled(x, left):
    turned = pltpu.roll(x, x.shape[1] // 2, 1)
    return jnp.where(left, x, turned), jnp.where(left, turned, x)


def far_kernel(
    far_index, up_index, near, own, beside, pair, pair_beside, side, side_beside, third,
    far_coupling, up_coupling, transfer, basis, base, held,
):
    leaves, rows, points = near.shape
    rank = basis.shape[1]
    half = rows // 2
    slots = [s for s in range(far_index.shape[1]) if s != PARTNER]
    here = lax.axis_index("leaf")
    left = lax.broadcasted_iota(jnp.int32, (half, 2 * rank), 1) < rank
    left_all = lax.broadcasted_iota(jnp.int32, (rows, 2 * rank), 1) < rank
    sources = (own, beside, pair, pair_beside, side, side_beside, third)
    for k, source in enumerate(sources):
        for i in range(leaves + 1):
            block = k * (leaves + 1) + i
            held[block, :half], held[block, half:] = doubled(source[i * half : (i + 1) * half], left)
    index = far_index[...]
    device = lax.div(index, leaves)
    places = place(device, here) * (leaves + 1) + (index - device * leaves)
    up_places = place(up_index[...], here) * (leaves + 1) + leaves

    def chosen(u, s):
        return held[places[u, s] if u < leaves else up_places[0, s]]

    def far(u, coupling):
        inputs = [jnp.where(left_all, chosen(u, s), chosen(u, t)) for s, t in zip(slots[0:-1:2], slots[1::2])]
        if len(slots) % 2:
            inputs.append(chosen(u, slots[-1])[:, :rank])
        return dot(jnp.concatenate(inputs, axis=1), jnp.concatenate([coupling[s] for s in slots], axis=0), NN)

    parent_far = far(leaves, up_coupling[0])
    down = dot(parent_far, transfer[...].reshape(leaves * rank, rank), NT)
    leaf_fars = [far(l, far_coupling[l]) for l in range(leaves)]
    for l in range(leaves):
        leaf_far = leaf_fars[l] + down[:, l * rank : (l + 1) * rank]
        base[l] = near[l] + dot(leaf_far, basis[l], NN)


def partner_kernel(base, opposite, high, low, product):
    leaves, rows, points = base.shape
    half = rows // 2
    left = lax.broadcasted_iota(jnp.int32, (half, points), 1) < points // 2
    blocks = [doubled(opposite[i * half : (i + 1) * half], left) for i in range(leaves + 1)]
    parent = blocks[leaves]
    for l in range(leaves):
        inputs = jnp.concatenate([jnp.where(left, blocks[l][i], parent[i]) for i in range(2)], axis=0)
        xh, xl = split(inputs)
        both = mul(jnp.concatenate([xh, xl], axis=0), high[l], NN)
        product[l] = base[l] + (both[:rows] + (both[rows:] + mul(xh, low[l], NN)))


def other_side(core):
    return core + 2 if core & 2 else core - 2


def routes(groups, count):
    last = count - 1
    ends = (0, 1, last - 1, last)

    def everywhere(pairs):
        return [(g * count + j, g * count + i) for g in range(groups) for j, i in pairs]

    def mirrored(step):
        wanted = [(i - step, i) if i % 2 == 0 else (i + step, i) for i in range(count)]
        return [(j, i) for j, i in wanted if 0 <= j <= last]

    beside = everywhere([(i ^ 1, i) for i in range(count)])
    pair = everywhere([(i ^ 2, i) for i in range(count)])
    opposite = everywhere([((i + count // 2) % count, i) for i in range(count)])
    third = everywhere(mirrored(3))
    across = everywhere(mirrored(1))
    side = everywhere([(i ^ 1 if i in ends else other_side(i), i) for i in range(count)])
    if groups > 1:
        across += [(g * count + i, (g + 1) % groups * count + i) for g in range(groups) for i in (0, last)]
        third += [(g * count + i, (g + 1) % groups * count + i) for g in range(groups) for i in (0, 2, last - 2, last)]
    return beside, across, pair, side, third, opposite


def per_device(
    groups, vectors, near_index, near_block, basis, far_index, far_coupling, transfer, up_index, up_coupling
):
    leaves, rows, points = vectors.shape
    rank = basis.shape[2]
    packed = (leaves + 1) * rows // 2
    basis = jnp.swapaxes(basis, 1, 2)
    beside_to, across_to, pair_to, side_to, third_to, opposite_to = routes(groups, lax.axis_size("leaf"))

    def send(x, to):
        return lax.ppermute(x, ("groups", "leaf"), to)

    vectors_across = send(vectors, across_to)
    vectors_beside = send(vectors, beside_to)
    own, own_longer = pl.pallas_call(
        coeffs_kernel,
        out_shape=tuple(jax.ShapeDtypeStruct((packed + extra, points), F32) for extra in (0, 8)),
        in_specs=[HBM] * 3,
        out_specs=(VMEM, VMEM),
        scratch_shapes=[
            pltpu.VMEM(vectors.shape, F32),
            pltpu.VMEM(basis.shape, F32),
            pltpu.VMEM(transfer.shape, F32),
            pltpu.SemaphoreType.DMA((3,)),
        ],
        compiler_params=room(4),
        cost_estimate=cost(5),
    )(*(pltpu.with_memory_space_constraint(x, pltpu.HBM) for x in (vectors, basis, transfer)))
    own, vectors_beside = lax.optimization_barrier((own, vectors_beside))
    pair = send(own, pair_to)
    side = send(own, side_to)
    opposite = send(own_longer, opposite_to)
    third = send(own, third_to)
    beside = send(own, beside_to)
    whole = jax.ShapeDtypeStruct(vectors.shape, F32)
    parts = jax.ShapeDtypeStruct((leaves, 2 * rank, points), jnp.bfloat16)
    vectors_across, side, pair = lax.optimization_barrier((vectors_across, side, pair))
    pair_beside = send(pair, beside_to)
    side_beside = send(side, beside_to)
    near = pl.pallas_call(
        near_kernel,
        out_shape=whole,
        in_specs=[VMEM] * 5,
        out_specs=VMEM,
        scratch_shapes=[pltpu.VMEM((3 * leaves, rows, points), F32)],
        compiler_params=room(8),
        cost_estimate=cost(0),
    )(near_index, near_block, vectors, vectors_beside, vectors_across)
    high, low = pl.pallas_call(
        partner_matrices_kernel,
        out_shape=(parts, parts),
        in_specs=[VMEM] * 4,
        out_specs=(VMEM, VMEM),
        compiler_params=room(4),
        cost_estimate=cost(3),
    )(far_coupling, up_coupling, transfer, basis)
    base = pl.pallas_call(
        far_kernel,
        out_shape=whole,
        in_specs=[VMEM] * 14,
        out_specs=VMEM,
        scratch_shapes=[pltpu.VMEM((7 * (leaves + 1), rows, points), F32)],
        compiler_params=room(10),
        cost_estimate=cost(0),
    )(
        far_index, up_index, near, own, beside, pair, pair_beside, side, side_beside, third,
        far_coupling, up_coupling, transfer, basis,
    )
    return pl.pallas_call(
        partner_kernel,
        out_shape=whole,
        in_specs=[VMEM] * 4,
        out_specs=VMEM,
        compiler_params=room(4),
        cost_estimate=cost(0),
    )(base, opposite, high, low)


def solution(mesh):
    placed = (
        P(("groups", "leaf"), None, None),
        P(("groups", "leaf"), None),
        P(("groups", "leaf"), None, None, None),
        P(("groups", "leaf"), None, None),
        P(("groups", "leaf"), None),
        P(("groups", "leaf"), None, None, None),
        P(("groups", "leaf"), None, None),
        P(("groups", "leaf"), None),
        P(("groups", "leaf"), None, None, None),
    )
    return jax.shard_map(
        functools.partial(per_device, mesh.shape["groups"]),
        mesh=mesh,
        in_specs=placed,
        out_specs=P(("groups", "leaf"), None, None),
        check_vma=False,
    )
```

```python
import functools

import jax
import jax.numpy as jnp
from jax import lax
from jax.experimental import pallas as pl
from jax.experimental.pallas import tpu as pltpu
from jax.sharding import PartitionSpec as P

PARTNER = 2
F32 = jnp.float32
NN = (((1,), (0,)), ((), ()))
NT = (((1,), (1,)), ((), ()))
HBM = pl.BlockSpec(memory_space=pltpu.HBM)
VMEM = pl.BlockSpec(memory_space=pltpu.VMEM)


def cost(us):
    return pl.CostEstimate(flops=us * 500_000_000, bytes_accessed=0, transcendentals=0)


def room(mib):
    return pltpu.CompilerParams(vmem_limit_bytes=mib << 20)


def split(x):
    high = x.astype(jnp.bfloat16)
    return high, (x - high.astype(F32)).astype(jnp.bfloat16)


def mul(x, y, dims):
    return lax.dot_general(x, y, dims, preferred_element_type=F32)


def dot(x, y, dims):
    rows = x.shape[0]
    xh, xl = split(x)
    yh, yl = split(y)
    both = mul(jnp.concatenate([xh, xl], axis=0), yh, dims)
    return both[:rows] + (both[rows:] + mul(xh, yl, dims))


def streamed(blocks, inputs):
    rows = inputs.shape[0]
    bh, bl = split(blocks)
    xh, xl = split(inputs)
    both = mul(bh, jnp.concatenate([xh, xl], axis=0), NT)
    return (both[:, :rows] + (both[:, rows:] + mul(bl, xh, NT))).T


def pack(x):
    half = x.shape[0] // 2
    return jnp.concatenate([x[:half], x[half:]], axis=1)


def coeffs_kernel(vectors, basis, transfer, coeffs, longer):
    leaves, rows, points = vectors.shape
    rank = basis.shape[1]
    half = rows // 2
    parts = []
    for l in range(leaves):
        parts.append(dot(vectors[l], basis[l], NT))
    whole = jnp.concatenate(parts, axis=1)
    parts.append(dot(whole, transfer[...].reshape(leaves * rank, rank), NN))
    for i, part in enumerate(parts):
        packed = pack(part)
        coeffs[i * half : (i + 1) * half] = packed
        longer[i * half : (i + 1) * half] = packed
    longer[len(parts) * half :] = jnp.zeros_like(longer[len(parts) * half :])


def place(index, here):
    differ = index ^ here
    side = (index ^ other_side_of(here)) & -2 == 0
    return jnp.where(differ & -4 == 0, differ, jnp.where(side, 4 + (differ & 1), 6))


def other_side_of(core):
    return core - 2 + 2 * (core & 2)


def near_kernel(near_index, near_block, own, beside, across, near, held):
    leaves, slots = near_index.shape
    rows = near.shape[1]
    here = lax.axis_index("leaf")
    side = 1 - 2 * lax.rem(here, 2)
    for l in range(leaves):
        held[l] = across[l]
        held[leaves + l] = own[l]
        held[2 * leaves + l] = beside[l]
    index = near_index[...]
    device = lax.div(index, leaves)
    places = ((device - here) * side + 1) * leaves + (index - device * leaves)
    for l in range(leaves):
        chosen = [held[places[l, s]] for s in range(slots)]
        inputs = jnp.concatenate(chosen, axis=1)
        blocks = jnp.concatenate([near_block[l, s] for s in range(slots)], axis=1)
        near[l] = streamed(blocks, inputs)


def partner_matrices_kernel(far_coupling, up_coupling, transfer, basis, high, low):
    leaves, rank, points = basis.shape
    through = dot(up_coupling[0, PARTNER], transfer[...].reshape(leaves * rank, rank), NT)
    for l in range(leaves):
        two = jnp.concatenate([far_coupling[l, PARTNER], through[:, l * rank : (l + 1) * rank]], axis=0)
        high[l], low[l] = split(dot(two, basis[l], NN))


def doubled(x, left):
    turned = pltpu.roll(x, x.shape[1] // 2, 1)
    return jnp.where(left, x, turned), jnp.where(left, turned, x)


def far_kernel(
    far_index, up_index, near, own, beside, pair, pair_beside, side, side_beside, third,
    far_coupling, up_coupling, transfer, basis, base, held,
):
    leaves, rows, points = near.shape
    rank = basis.shape[1]
    half = rows // 2
    slots = [s for s in range(far_index.shape[1]) if s != PARTNER]
    here = lax.axis_index("leaf")
    left = lax.broadcasted_iota(jnp.int32, (half, 2 * rank), 1) < rank
    left_all = lax.broadcasted_iota(jnp.int32, (rows, 2 * rank), 1) < rank
    sources = (own, beside, pair, pair_beside, side, side_beside, third)
    for k, source in enumerate(sources):
        for i in range(leaves + 1):
            block = k * (leaves + 1) + i
            held[block, :half], held[block, half:] = doubled(source[i * half : (i + 1) * half], left)
    index = far_index[...]
    device = lax.div(index, leaves)
    places = place(device, here) * (leaves + 1) + (index - device * leaves)
    up_places = place(up_index[...], here) * (leaves + 1) + leaves

    def chosen(u, s):
        return held[places[u, s] if u < leaves else up_places[0, s]]

    def far(u, coupling):
        inputs = [jnp.where(left_all, chosen(u, s), chosen(u, t)) for s, t in zip(slots[0:-1:2], slots[1::2])]
        if len(slots) % 2:
            inputs.append(chosen(u, slots[-1])[:, :rank])
        return dot(jnp.concatenate(inputs, axis=1), jnp.concatenate([coupling[s] for s in slots], axis=0), NN)

    parent_far = far(leaves, up_coupling[0])
    down = dot(parent_far, transfer[...].reshape(leaves * rank, rank), NT)
    leaf_fars = [far(l, far_coupling[l]) for l in range(leaves)]
    for l in range(leaves):
        leaf_far = leaf_fars[l] + down[:, l * rank : (l + 1) * rank]
        base[l] = near[l] + dot(leaf_far, basis[l], NN)


def partner_kernel(base, opposite, high, low, product):
    leaves, rows, points = base.shape
    half = rows // 2
    left = lax.broadcasted_iota(jnp.int32, (half, points), 1) < points // 2
    blocks = [doubled(opposite[i * half : (i + 1) * half], left) for i in range(leaves + 1)]
    parent = blocks[leaves]
    for l in range(leaves):
        inputs = jnp.concatenate([jnp.where(left, blocks[l][i], parent[i]) for i in range(2)], axis=0)
        xh, xl = split(inputs)
        both = mul(jnp.concatenate([xh, xl], axis=0), high[l], NN)
        product[l] = base[l] + (both[:rows] + (both[rows:] + mul(xh, low[l], NN)))


def other_side(core):
    return core + 2 if core & 2 else core - 2


def routes(groups, count):
    last = count - 1
    ends = (0, 1, last - 1, last)

    def everywhere(pairs):
        return [(g * count + j, g * count + i) for g in range(groups) for j, i in pairs]

    def mirrored(step):
        sources = [i - step if i % 2 == 0 else i + step for i in range(count)]
        return [(j if 0 <= j <= last else i ^ 1, i) for i, j in enumerate(sources)]

    beside = everywhere([(i ^ 1, i) for i in range(count)])
    pair = everywhere([(i ^ 2, i) for i in range(count)])
    opposite = everywhere([((i + count // 2) % count ^ 1, i) for i in range(count)])
    third = everywhere(mirrored(4))
    across = everywhere([(i - 1 if i % 2 == 0 else i + 1, i) for i in range(count) if i not in (0, last)])
    side = everywhere([(i ^ 1 if i in ends else other_side(i), i) for i in range(count)])
    if groups > 1:
        across += [(g * count + i, (g + 1) % groups * count + i) for g in range(groups) for i in (0, last)]
    return beside, across, pair, side, third, opposite


def per_device(
    groups, vectors, near_index, near_block, basis, far_index, far_coupling, transfer, up_index, up_coupling
):
    leaves, rows, points = vectors.shape
    rank = basis.shape[2]
    packed = (leaves + 1) * rows // 2
    basis = jnp.swapaxes(basis, 1, 2)
    beside_to, across_to, pair_to, side_to, third_to, opposite_to = routes(groups, lax.axis_size("leaf"))

    def send(x, to):
        return lax.ppermute(x, ("groups", "leaf"), to)

    basis_beside = send(basis, beside_to)
    transfer_beside = send(transfer, beside_to)
    vectors_beside = send(vectors, beside_to)
    vectors_across = send(vectors, across_to)
    theirs, theirs_longer = pl.pallas_call(
        coeffs_kernel,
        out_shape=tuple(jax.ShapeDtypeStruct((packed + extra, points), F32) for extra in (0, 8)),
        in_specs=[VMEM] * 3,
        out_specs=(VMEM, VMEM),
        compiler_params=room(4),
        cost_estimate=cost(5),
    )(vectors_beside, basis_beside, transfer_beside)
    pair = send(theirs, pair_to)
    side = send(theirs, side_to)
    opposite = send(theirs_longer, opposite_to)
    third = send(theirs, third_to)
    own = send(theirs, beside_to)
    whole = jax.ShapeDtypeStruct(vectors.shape, F32)
    parts = jax.ShapeDtypeStruct((leaves, 2 * rank, points), jnp.bfloat16)
    vectors_across, pair, side = lax.optimization_barrier((vectors_across, pair, side))
    pair_beside = send(pair, beside_to)
    side_beside = send(side, beside_to)
    near = pl.pallas_call(
        near_kernel,
        out_shape=whole,
        in_specs=[VMEM] * 5,
        out_specs=VMEM,
        scratch_shapes=[pltpu.VMEM((3 * leaves, rows, points), F32)],
        compiler_params=room(8),
        cost_estimate=cost(0),
    )(near_index, near_block, vectors, vectors_beside, vectors_across)
    high, low = pl.pallas_call(
        partner_matrices_kernel,
        out_shape=(parts, parts),
        in_specs=[VMEM] * 4,
        out_specs=(VMEM, VMEM),
        compiler_params=room(4),
        cost_estimate=cost(0),
    )(far_coupling, up_coupling, transfer, basis)
    base = pl.pallas_call(
        far_kernel,
        out_shape=whole,
        in_specs=[VMEM] * 14,
        out_specs=VMEM,
        scratch_shapes=[pltpu.VMEM((7 * (leaves + 1), rows, points), F32)],
        compiler_params=room(10),
        cost_estimate=cost(0),
    )(
        far_index, up_index, near, own, theirs, pair_beside, pair, side_beside, side, third,
        far_coupling, up_coupling, transfer, basis,
    )
    return pl.pallas_call(
        partner_kernel,
        out_shape=whole,
        in_specs=[VMEM] * 4,
        out_specs=VMEM,
        compiler_params=room(4),
        cost_estimate=cost(0),
    )(base, opposite, high, low)


def solution(mesh):
    placed = (
        P(("groups", "leaf"), None, None),
        P(("groups", "leaf"), None),
        P(("groups", "leaf"), None, None, None),
        P(("groups", "leaf"), None, None),
        P(("groups", "leaf"), None),
        P(("groups", "leaf"), None, None, None),
        P(("groups", "leaf"), None, None),
        P(("groups", "leaf"), None),
        P(("groups", "leaf"), None, None, None),
    )
    return jax.shard_map(
        functools.partial(per_device, mesh.shape["groups"]),
        mesh=mesh,
        in_specs=placed,
        out_specs=P(("groups", "leaf"), None, None),
        check_vma=False,
    )
```

```python
import functools

import jax
import jax.numpy as jnp
from jax import lax
from jax.experimental import pallas as pl
from jax.experimental.pallas import tpu as pltpu
from jax.sharding import PartitionSpec as P

PARTNER = 2
F32 = jnp.float32
NN = (((1,), (0,)), ((), ()))
NT = (((1,), (1,)), ((), ()))
HBM = pl.BlockSpec(memory_space=pltpu.HBM)
VMEM = pl.BlockSpec(memory_space=pltpu.VMEM)


def cost(us):
    return pl.CostEstimate(flops=us * 500_000_000, bytes_accessed=0, transcendentals=0)


def room(mib):
    return pltpu.CompilerParams(vmem_limit_bytes=mib << 20)


def split(x):
    high = x.astype(jnp.bfloat16)
    return high, (x - high.astype(F32)).astype(jnp.bfloat16)


def mul(x, y, dims):
    return lax.dot_general(x, y, dims, preferred_element_type=F32)


def dot(x, y, dims):
    rows = x.shape[0]
    xh, xl = split(x)
    yh, yl = split(y)
    both = mul(jnp.concatenate([xh, xl], axis=0), yh, dims)
    return both[:rows] + (both[rows:] + mul(xh, yl, dims))


def streamed(blocks, inputs):
    rows = inputs.shape[0]
    bh, bl = split(blocks)
    xh, xl = split(inputs)
    both = mul(bh, jnp.concatenate([xh, xl], axis=0), NT)
    return (both[:, :rows] + (both[:, rows:] + mul(bl, xh, NT))).T


def pack(x):
    half = x.shape[0] // 2
    return jnp.concatenate([x[:half], x[half:]], axis=1)


def coeffs_kernel(vectors, basis, transfer, coeffs, longer):
    leaves, rows, points = vectors.shape
    rank = basis.shape[1]
    half = rows // 2
    parts = []
    for l in range(leaves):
        parts.append(dot(vectors[l], basis[l], NT))
    whole = jnp.concatenate(parts, axis=1)
    parts.append(dot(whole, transfer[...].reshape(leaves * rank, rank), NN))
    for i, part in enumerate(parts):
        packed = pack(part)
        coeffs[i * half : (i + 1) * half] = packed
        longer[i * half : (i + 1) * half] = packed
    longer[len(parts) * half :] = jnp.zeros_like(longer[len(parts) * half :])


def place(index, here):
    differ = index ^ here
    side = (index ^ other_side_of(here)) & -2 == 0
    return jnp.where(differ & -4 == 0, differ, jnp.where(side, 4 + (differ & 1), 6))


def other_side_of(core):
    return core - 2 + 2 * (core & 2)


def near_kernel(near_index, near_block, own, beside, across, near, held):
    leaves, slots = near_index.shape
    rows = near.shape[1]
    here = lax.axis_index("leaf")
    side = 1 - 2 * lax.rem(here, 2)
    for l in range(leaves):
        held[l] = across[l]
        held[leaves + l] = own[l]
        held[2 * leaves + l] = beside[l]
    index = near_index[...]
    device = lax.div(index, leaves)
    places = ((device - here) * side + 1) * leaves + (index - device * leaves)
    for l in range(leaves):
        chosen = [held[places[l, s]] for s in range(slots)]
        inputs = jnp.concatenate(chosen, axis=1)
        blocks = jnp.concatenate([near_block[l, s] for s in range(slots)], axis=1)
        near[l] = streamed(blocks, inputs)


def partner_matrices_kernel(far_coupling, up_coupling, transfer, basis, high, low):
    leaves, rank, points = basis.shape
    through = dot(up_coupling[0, PARTNER], transfer[...].reshape(leaves * rank, rank), NT)
    for l in range(leaves):
        two = jnp.concatenate([far_coupling[l, PARTNER], through[:, l * rank : (l + 1) * rank]], axis=0)
        high[l], low[l] = split(dot(two, basis[l], NN))


def doubled(x, left):
    turned = pltpu.roll(x, x.shape[1] // 2, 1)
    return jnp.where(left, x, turned), jnp.where(left, turned, x)


def far_kernel(
    far_index, up_index, near, own, beside, pair, pair_beside, side, side_beside, third,
    far_coupling, up_coupling, transfer, basis, base, held,
):
    leaves, rows, points = near.shape
    rank = basis.shape[1]
    half = rows // 2
    slots = [s for s in range(far_index.shape[1]) if s != PARTNER]
    here = lax.axis_index("leaf")
    left = lax.broadcasted_iota(jnp.int32, (half, 2 * rank), 1) < rank
    left_all = lax.broadcasted_iota(jnp.int32, (rows, 2 * rank), 1) < rank
    sources = (own, beside, pair, pair_beside, side, side_beside, third)
    for k, source in enumerate(sources):
        for i in range(leaves + 1):
            block = k * (leaves + 1) + i
            held[block, :half], held[block, half:] = doubled(source[i * half : (i + 1) * half], left)
    index = far_index[...]
    device = lax.div(index, leaves)
    places = place(device, here) * (leaves + 1) + (index - device * leaves)
    up_places = place(up_index[...], here) * (leaves + 1) + leaves

    def chosen(u, s):
        return held[places[u, s] if u < leaves else up_places[0, s]]

    def far(u, coupling):
        inputs = [jnp.where(left_all, chosen(u, s), chosen(u, t)) for s, t in zip(slots[0:-1:2], slots[1::2])]
        if len(slots) % 2:
            inputs.append(chosen(u, slots[-1])[:, :rank])
        return dot(jnp.concatenate(inputs, axis=1), jnp.concatenate([coupling[s] for s in slots], axis=0), NN)

    parent_far = far(leaves, up_coupling[0])
    down = dot(parent_far, transfer[...].reshape(leaves * rank, rank), NT)
    leaf_fars = [far(l, far_coupling[l]) for l in range(leaves)]
    for l in range(leaves):
        leaf_far = leaf_fars[l] + down[:, l * rank : (l + 1) * rank]
        base[l] = near[l] + dot(leaf_far, basis[l], NN)


def partner_kernel(base, opposite, high, low, product):
    leaves, rows, points = base.shape
    half = rows // 2
    left = lax.broadcasted_iota(jnp.int32, (half, points), 1) < points // 2
    blocks = [doubled(opposite[i * half : (i + 1) * half], left) for i in range(leaves + 1)]
    parent = blocks[leaves]
    for l in range(leaves):
        inputs = jnp.concatenate([jnp.where(left, blocks[l][i], parent[i]) for i in range(2)], axis=0)
        xh, xl = split(inputs)
        both = mul(jnp.concatenate([xh, xl], axis=0), high[l], NN)
        product[l] = base[l] + (both[:rows] + (both[rows:] + mul(xh, low[l], NN)))


def other_side(core):
    return core + 2 if core & 2 else core - 2


def routes(groups, count):
    last = count - 1
    ends = (0, 1, last - 1, last)

    def everywhere(pairs):
        return [(g * count + j, g * count + i) for g in range(groups) for j, i in pairs]

    def mirrored(step):
        sources = [i - step if i % 2 == 0 else i + step for i in range(count)]
        return [(j if 0 <= j <= last else i ^ 1, i) for i, j in enumerate(sources)]

    beside = everywhere([(i ^ 1, i) for i in range(count)])
    pair = everywhere([(i ^ 2, i) for i in range(count)])
    opposite = everywhere([((i + count // 2) % count ^ 1, i) for i in range(count)])
    third = everywhere(mirrored(4))
    across = everywhere([(i - 1 if i % 2 == 0 else i + 1, i) for i in range(count) if i not in (0, last)])
    side = everywhere([(i ^ 1 if i in ends else other_side(i), i) for i in range(count)])
    if groups > 1:
        across += [(g * count + i, (g + 1) % groups * count + i) for g in range(groups) for i in (0, last)]
    return beside, across, pair, side, third, opposite


def per_device(
    groups, vectors, near_index, near_block, basis, far_index, far_coupling, transfer, up_index, up_coupling
):
    leaves, rows, points = vectors.shape
    rank = basis.shape[2]
    packed = (leaves + 1) * rows // 2
    basis = jnp.swapaxes(basis, 1, 2)
    beside_to, across_to, pair_to, side_to, third_to, opposite_to = routes(groups, lax.axis_size("leaf"))

    def send(x, to):
        return lax.ppermute(x, ("groups", "leaf"), to)

    basis_beside = send(basis, beside_to)
    transfer_beside = send(transfer, beside_to)
    vectors_beside = send(vectors, beside_to)
    vectors_across = send(vectors, across_to)
    theirs, theirs_longer = pl.pallas_call(
        coeffs_kernel,
        out_shape=tuple(jax.ShapeDtypeStruct((packed + extra, points), F32) for extra in (0, 8)),
        in_specs=[VMEM] * 3,
        out_specs=(VMEM, VMEM),
        compiler_params=room(4),
        cost_estimate=cost(5),
    )(vectors_beside, basis_beside, transfer_beside)
    pair = send(theirs, pair_to)
    side = send(theirs, side_to)
    opposite = send(theirs_longer, opposite_to)
    third = send(theirs, third_to)
    own = send(theirs_longer, beside_to)
    whole = jax.ShapeDtypeStruct(vectors.shape, F32)
    parts = jax.ShapeDtypeStruct((leaves, 2 * rank, points), jnp.bfloat16)
    high, low = pl.pallas_call(
        partner_matrices_kernel,
        out_shape=(parts, parts),
        in_specs=[VMEM] * 4,
        out_specs=(VMEM, VMEM),
        compiler_params=room(4),
        cost_estimate=cost(0),
    )(far_coupling, up_coupling, transfer, basis)
    vectors_across, side, pair, high, low = lax.optimization_barrier((vectors_across, side, pair, high, low))
    pair_beside = send(pair, beside_to)
    side_beside = send(side, beside_to)
    near = pl.pallas_call(
        near_kernel,
        out_shape=whole,
        in_specs=[VMEM] * 5,
        out_specs=VMEM,
        scratch_shapes=[pltpu.VMEM((3 * leaves, rows, points), F32)],
        compiler_params=room(8),
        cost_estimate=cost(0),
    )(near_index, near_block, vectors, vectors_beside, vectors_across)
    base = pl.pallas_call(
        far_kernel,
        out_shape=whole,
        in_specs=[VMEM] * 14,
        out_specs=VMEM,
        scratch_shapes=[pltpu.VMEM((7 * (leaves + 1), rows, points), F32)],
        compiler_params=room(10),
        cost_estimate=cost(0),
    )(
        far_index, up_index, near, own, theirs, pair_beside, pair, side_beside, side, third,
        far_coupling, up_coupling, transfer, basis,
    )
    return pl.pallas_call(
        partner_kernel,
        out_shape=whole,
        in_specs=[VMEM] * 4,
        out_specs=VMEM,
        compiler_params=room(4),
        cost_estimate=cost(0),
    )(base, opposite, high, low)


def solution(mesh):
    placed = (
        P(("groups", "leaf"), None, None),
        P(("groups", "leaf"), None),
        P(("groups", "leaf"), None, None, None),
        P(("groups", "leaf"), None, None),
        P(("groups", "leaf"), None),
        P(("groups", "leaf"), None, None, None),
        P(("groups", "leaf"), None, None),
        P(("groups", "leaf"), None),
        P(("groups", "leaf"), None, None, None),
    )
    return jax.shard_map(
        functools.partial(per_device, mesh.shape["groups"]),
        mesh=mesh,
        in_specs=placed,
        out_specs=P(("groups", "leaf"), None, None),
        check_vma=False,
    )
```

```python
import functools

import jax
import jax.numpy as jnp
from jax import lax
from jax.experimental import pallas as pl
from jax.experimental.pallas import tpu as pltpu
from jax.sharding import PartitionSpec as P

PARTNER = 2
F32 = jnp.float32
NN = (((1,), (0,)), ((), ()))
NT = (((1,), (1,)), ((), ()))
HBM = pl.BlockSpec(memory_space=pltpu.HBM)
VMEM = pl.BlockSpec(memory_space=pltpu.VMEM)


def cost(us):
    return pl.CostEstimate(flops=us * 500_000_000, bytes_accessed=0, transcendentals=0)


def room(mib):
    return pltpu.CompilerParams(vmem_limit_bytes=mib << 20)


def split(x):
    high = x.astype(jnp.bfloat16)
    return high, (x - high.astype(F32)).astype(jnp.bfloat16)


def mul(x, y, dims):
    return lax.dot_general(x, y, dims, preferred_element_type=F32)


def dot(x, y, dims):
    rows = x.shape[0]
    xh, xl = split(x)
    yh, yl = split(y)
    both = mul(jnp.concatenate([xh, xl], axis=0), yh, dims)
    return both[:rows] + (both[rows:] + mul(xh, yl, dims))


def streamed(blocks, inputs):
    rows = inputs.shape[0]
    bh, bl = split(blocks)
    xh, xl = split(inputs)
    both = mul(bh, jnp.concatenate([xh, xl], axis=0), NT)
    return (both[:, :rows] + (both[:, rows:] + mul(bl, xh, NT))).T


def pack(x):
    half = x.shape[0] // 2
    return jnp.concatenate([x[:half], x[half:]], axis=1)


def coeffs_kernel(vectors, basis, transfer, coeffs, *longer):
    leaves, rows, points = vectors.shape
    rank = basis.shape[1]
    half = rows // 2
    parts = []
    for l in range(leaves):
        parts.append(dot(vectors[l], basis[l], NT))
    whole = jnp.concatenate(parts, axis=1)
    parts.append(dot(whole, transfer[...].reshape(leaves * rank, rank), NN))
    for i, part in enumerate(parts):
        packed = pack(part)
        coeffs[i * half : (i + 1) * half] = packed
        for out in longer:
            out[i * half : (i + 1) * half] = packed
    for out in longer:
        out[len(parts) * half :] = jnp.zeros_like(out[len(parts) * half :])


def place(index, here):
    differ = index ^ here
    side = (index ^ other_side_of(here)) & -2 == 0
    return jnp.where(differ & -4 == 0, jnp.maximum(differ - 1, 0), jnp.where(side, 3 + (differ & 1), 5))


def other_side_of(core):
    return core - 2 + 2 * (core & 2)


def near_kernel(near_index, near_block, own, beside, across, near, held):
    leaves, slots = near_index.shape
    rows = near.shape[1]
    here = lax.axis_index("leaf")
    side = 1 - 2 * lax.rem(here, 2)
    for l in range(leaves):
        held[l] = across[l]
        held[leaves + l] = own[l]
        held[2 * leaves + l] = beside[l]
    index = near_index[...]
    device = lax.div(index, leaves)
    places = ((device - here) * side + 1) * leaves + (index - device * leaves)
    for l in range(leaves):
        chosen = [held[places[l, s]] for s in range(slots)]
        inputs = jnp.concatenate(chosen, axis=1)
        blocks = jnp.concatenate([near_block[l, s] for s in range(slots)], axis=1)
        near[l] = streamed(blocks, inputs)


def partner_matrices_kernel(far_coupling, up_coupling, transfer, basis, high, low):
    leaves, rank, points = basis.shape
    through = dot(up_coupling[0, PARTNER], transfer[...].reshape(leaves * rank, rank), NT)
    for l in range(leaves):
        two = jnp.concatenate([far_coupling[l, PARTNER], through[:, l * rank : (l + 1) * rank]], axis=0)
        high[l], low[l] = split(dot(two, basis[l], NN))


def doubled(x, left):
    turned = pltpu.roll(x, x.shape[1] // 2, 1)
    return jnp.where(left, x, turned), jnp.where(left, turned, x)


def far_kernel(
    far_index, up_index, near, beside, pair, pair_beside, side, side_beside, third,
    far_coupling, up_coupling, transfer, basis, base, held,
):
    leaves, rows, points = near.shape
    rank = basis.shape[1]
    half = rows // 2
    slots = [s for s in range(far_index.shape[1]) if s != PARTNER]
    here = lax.axis_index("leaf")
    left = lax.broadcasted_iota(jnp.int32, (half, 2 * rank), 1) < rank
    left_all = lax.broadcasted_iota(jnp.int32, (rows, 2 * rank), 1) < rank
    sources = (beside, pair, pair_beside, side, side_beside, third)
    for k, source in enumerate(sources):
        for i in range(leaves + 1):
            block = k * (leaves + 1) + i
            held[block, :half], held[block, half:] = doubled(source[i * half : (i + 1) * half], left)
    index = far_index[...]
    device = lax.div(index, leaves)
    places = place(device, here) * (leaves + 1) + (index - device * leaves)
    up_places = place(up_index[...], here) * (leaves + 1) + leaves

    def chosen(u, s):
        return held[places[u, s] if u < leaves else up_places[0, s]]

    def far(u, coupling):
        inputs = [jnp.where(left_all, chosen(u, s), chosen(u, t)) for s, t in zip(slots[0:-1:2], slots[1::2])]
        if len(slots) % 2:
            inputs.append(chosen(u, slots[-1])[:, :rank])
        return dot(jnp.concatenate(inputs, axis=1), jnp.concatenate([coupling[s] for s in slots], axis=0), NN)

    parent_far = far(leaves, up_coupling[0])
    down = dot(parent_far, transfer[...].reshape(leaves * rank, rank), NT)
    leaf_fars = [far(l, far_coupling[l]) for l in range(leaves)]
    for l in range(leaves):
        leaf_far = leaf_fars[l] + down[:, l * rank : (l + 1) * rank]
        base[l] = near[l] + dot(leaf_far, basis[l], NN)


def partner_kernel(base, opposite, high, low, product):
    leaves, rows, points = base.shape
    half = rows // 2
    left = lax.broadcasted_iota(jnp.int32, (half, points), 1) < points // 2
    blocks = [doubled(opposite[i * half : (i + 1) * half], left) for i in range(leaves + 1)]
    parent = blocks[leaves]
    for l in range(leaves):
        inputs = jnp.concatenate([jnp.where(left, blocks[l][i], parent[i]) for i in range(2)], axis=0)
        xh, xl = split(inputs)
        both = mul(jnp.concatenate([xh, xl], axis=0), high[l], NN)
        product[l] = base[l] + (both[:rows] + (both[rows:] + mul(xh, low[l], NN)))


def other_side(core):
    return core + 2 if core & 2 else core - 2


def routes(groups, count):
    last = count - 1
    ends = (0, 1, last - 1, last)

    def everywhere(pairs):
        return [(g * count + j, g * count + i) for g in range(groups) for j, i in pairs]

    def mirrored(step):
        sources = [i - step if i % 2 == 0 else i + step for i in range(count)]
        return [(j if 0 <= j <= last else i ^ 1, i) for i, j in enumerate(sources)]

    beside = everywhere([(i ^ 1, i) for i in range(count)])
    pair = everywhere([(i ^ 2, i) for i in range(count)])
    opposite = everywhere([((i + count // 2) % count ^ 1, i) for i in range(count)])
    third = everywhere(mirrored(4))
    across = everywhere([(i - 1 if i % 2 == 0 else i + 1, i) for i in range(count) if i not in (0, last)])
    side = everywhere([(i ^ 1 if i in ends else other_side(i), i) for i in range(count)])
    if groups > 1:
        across += [(g * count + i, (g + 1) % groups * count + i) for g in range(groups) for i in (0, last)]
    return beside, across, pair, side, third, opposite


def per_device(
    groups, vectors, near_index, near_block, basis, far_index, far_coupling, transfer, up_index, up_coupling
):
    leaves, rows, points = vectors.shape
    rank = basis.shape[2]
    packed = (leaves + 1) * rows // 2
    basis = jnp.swapaxes(basis, 1, 2)
    beside_to, across_to, pair_to, side_to, third_to, opposite_to = routes(groups, lax.axis_size("leaf"))

    def send(x, to):
        return lax.ppermute(x, ("groups", "leaf"), to)

    basis_beside = send(basis, beside_to)
    transfer_beside = send(transfer, beside_to)
    vectors_beside = send(vectors, beside_to)
    vectors_across = send(vectors, across_to)
    theirs, theirs_longer, theirs_longest = pl.pallas_call(
        coeffs_kernel,
        out_shape=tuple(jax.ShapeDtypeStruct((packed + extra, points), F32) for extra in (0, 8, 16)),
        in_specs=[VMEM] * 3,
        out_specs=(VMEM,) * 3,
        compiler_params=room(4),
        cost_estimate=cost(5),
    )(vectors_beside, basis_beside, transfer_beside)
    pair = send(theirs, pair_to)
    side = send(theirs, side_to)
    opposite = send(theirs_longest, opposite_to)
    third = send(theirs_longer, third_to)
    whole = jax.ShapeDtypeStruct(vectors.shape, F32)
    parts = jax.ShapeDtypeStruct((leaves, 2 * rank, points), jnp.bfloat16)
    high, low = pl.pallas_call(
        partner_matrices_kernel,
        out_shape=(parts, parts),
        in_specs=[VMEM] * 4,
        out_specs=(VMEM, VMEM),
        compiler_params=room(4),
        cost_estimate=cost(0),
    )(far_coupling, up_coupling, transfer, basis)
    vectors_across, side, pair, high, low = lax.optimization_barrier((vectors_across, side, pair, high, low))
    pair_beside = send(pair, beside_to)
    side_beside = send(side, beside_to)
    near = pl.pallas_call(
        near_kernel,
        out_shape=whole,
        in_specs=[VMEM] * 5,
        out_specs=VMEM,
        scratch_shapes=[pltpu.VMEM((3 * leaves, rows, points), F32)],
        compiler_params=room(8),
        cost_estimate=cost(0),
    )(near_index, near_block, vectors, vectors_beside, vectors_across)
    base = pl.pallas_call(
        far_kernel,
        out_shape=whole,
        in_specs=[VMEM] * 13,
        out_specs=VMEM,
        scratch_shapes=[pltpu.VMEM((6 * (leaves + 1), rows, points), F32)],
        compiler_params=room(10),
        cost_estimate=cost(0),
    )(
        far_index, up_index, near, theirs, pair_beside, pair, side_beside, side, third,
        far_coupling, up_coupling, transfer, basis,
    )
    return pl.pallas_call(
        partner_kernel,
        out_shape=whole,
        in_specs=[VMEM] * 4,
        out_specs=VMEM,
        compiler_params=room(4),
        cost_estimate=cost(0),
    )(base, opposite, high, low)


def solution(mesh):
    placed = (
        P(("groups", "leaf"), None, None),
        P(("groups", "leaf"), None),
        P(("groups", "leaf"), None, None, None),
        P(("groups", "leaf"), None, None),
        P(("groups", "leaf"), None),
        P(("groups", "leaf"), None, None, None),
        P(("groups", "leaf"), None, None),
        P(("groups", "leaf"), None),
        P(("groups", "leaf"), None, None, None),
    )
    return jax.shard_map(
        functools.partial(per_device, mesh.shape["groups"]),
        mesh=mesh,
        in_specs=placed,
        out_specs=P(("groups", "leaf"), None, None),
        check_vma=False,
    )
```

```python
import functools

import jax
import jax.numpy as jnp
from jax import lax
from jax.experimental import pallas as pl
from jax.experimental.pallas import tpu as pltpu
from jax.sharding import PartitionSpec as P

PARTNER = 2
F32 = jnp.float32
NN = (((1,), (0,)), ((), ()))
NT = (((1,), (1,)), ((), ()))
HBM = pl.BlockSpec(memory_space=pltpu.HBM)
VMEM = pl.BlockSpec(memory_space=pltpu.VMEM)


def cost(us):
    return pl.CostEstimate(flops=us * 500_000_000, bytes_accessed=0, transcendentals=0)


def room(mib):
    return pltpu.CompilerParams(vmem_limit_bytes=mib << 20)


def split(x):
    high = x.astype(jnp.bfloat16)
    return high, (x - high.astype(F32)).astype(jnp.bfloat16)


def mul(x, y, dims):
    return lax.dot_general(x, y, dims, preferred_element_type=F32)


def dot(x, y, dims):
    rows = x.shape[0]
    xh, xl = split(x)
    yh, yl = split(y)
    both = mul(jnp.concatenate([xh, xl], axis=0), yh, dims)
    return both[:rows] + (both[rows:] + mul(xh, yl, dims))


def streamed(blocks, inputs):
    rows = inputs.shape[0]
    bh, bl = split(blocks)
    xh, xl = split(inputs)
    both = mul(bh, jnp.concatenate([xh, xl], axis=0), NT)
    return (both[:, :rows] + (both[:, rows:] + mul(bl, xh, NT))).T


def pack(x):
    half = x.shape[0] // 2
    return jnp.concatenate([x[:half], x[half:]], axis=1)


def coeffs_kernel(vectors, basis, transfer, coeffs, *longer):
    leaves, rows, points = vectors.shape
    rank = basis.shape[1]
    half = rows // 2
    parts = []
    for l in range(leaves):
        parts.append(dot(vectors[l], basis[l], NT))
    whole = jnp.concatenate(parts, axis=1)
    parts.append(dot(whole, transfer[...].reshape(leaves * rank, rank), NN))
    for i, part in enumerate(parts):
        packed = pack(part)
        coeffs[i * half : (i + 1) * half] = packed
        for out in longer:
            out[i * half : (i + 1) * half] = packed
    for out in longer:
        out[len(parts) * half :] = jnp.zeros_like(out[len(parts) * half :])


def place(index, here):
    differ = index ^ here
    side = (index ^ other_side_of(here)) & -2 == 0
    return jnp.where(differ & -4 == 0, differ, jnp.where(side, 4 + (differ & 1), 6))


def other_side_of(core):
    return core - 2 + 2 * (core & 2)


def near_kernel(near_index, near_block, own, beside, across, near, held):
    leaves, slots = near_index.shape
    rows = near.shape[1]
    here = lax.axis_index("leaf")
    side = 1 - 2 * lax.rem(here, 2)
    for l in range(leaves):
        held[l] = across[l]
        held[leaves + l] = own[l]
        held[2 * leaves + l] = beside[l]
    index = near_index[...]
    device = lax.div(index, leaves)
    places = ((device - here) * side + 1) * leaves + (index - device * leaves)
    for l in range(leaves):
        chosen = [held[places[l, s]] for s in range(slots)]
        inputs = jnp.concatenate(chosen, axis=1)
        blocks = jnp.concatenate([near_block[l, s] for s in range(slots)], axis=1)
        near[l] = streamed(blocks, inputs)


def partner_matrices_kernel(far_coupling, up_coupling, transfer, basis, high, low):
    leaves, rank, points = basis.shape
    through = dot(up_coupling[0, PARTNER], transfer[...].reshape(leaves * rank, rank), NT)
    for l in range(leaves):
        two = jnp.concatenate([far_coupling[l, PARTNER], through[:, l * rank : (l + 1) * rank]], axis=0)
        high[l], low[l] = split(dot(two, basis[l], NN))


def doubled(x, left):
    turned = pltpu.roll(x, x.shape[1] // 2, 1)
    return jnp.where(left, x, turned), jnp.where(left, turned, x)


def far_kernel(
    far_index, up_index, near, own, beside, pair, pair_beside, side, side_beside, third,
    far_coupling, up_coupling, transfer, basis, base, held,
):
    leaves, rows, points = near.shape
    rank = basis.shape[1]
    half = rows // 2
    slots = [s for s in range(far_index.shape[1]) if s != PARTNER]
    here = lax.axis_index("leaf")
    left = lax.broadcasted_iota(jnp.int32, (half, 2 * rank), 1) < rank
    left_all = lax.broadcasted_iota(jnp.int32, (rows, 2 * rank), 1) < rank
    sources = (own, beside, pair, pair_beside, side, side_beside, third)
    for k, source in enumerate(sources):
        for i in range(leaves + 1):
            block = k * (leaves + 1) + i
            held[block, :half], held[block, half:] = doubled(source[i * half : (i + 1) * half], left)
    index = far_index[...]
    device = lax.div(index, leaves)
    places = place(device, here) * (leaves + 1) + (index - device * leaves)
    up_places = place(up_index[...], here) * (leaves + 1) + leaves

    def chosen(u, s):
        return held[places[u, s] if u < leaves else up_places[0, s]]

    def far(u, coupling):
        inputs = [jnp.where(left_all, chosen(u, s), chosen(u, t)) for s, t in zip(slots[0:-1:2], slots[1::2])]
        if len(slots) % 2:
            inputs.append(chosen(u, slots[-1])[:, :rank])
        return dot(jnp.concatenate(inputs, axis=1), jnp.concatenate([coupling[s] for s in slots], axis=0), NN)

    parent_far = far(leaves, up_coupling[0])
    down = dot(parent_far, transfer[...].reshape(leaves * rank, rank), NT)
    leaf_fars = [far(l, far_coupling[l]) for l in range(leaves)]
    for l in range(leaves):
        leaf_far = leaf_fars[l] + down[:, l * rank : (l + 1) * rank]
        base[l] = near[l] + dot(leaf_far, basis[l], NN)


def partner_kernel(base, opposite, high, low, product):
    leaves, rows, points = base.shape
    half = rows // 2
    left = lax.broadcasted_iota(jnp.int32, (half, points), 1) < points // 2
    blocks = [doubled(opposite[i * half : (i + 1) * half], left) for i in range(leaves + 1)]
    parent = blocks[leaves]
    for l in range(leaves):
        inputs = jnp.concatenate([jnp.where(left, blocks[l][i], parent[i]) for i in range(2)], axis=0)
        xh, xl = split(inputs)
        both = mul(jnp.concatenate([xh, xl], axis=0), high[l], NN)
        product[l] = base[l] + (both[:rows] + (both[rows:] + mul(xh, low[l], NN)))


def other_side(core):
    return core + 2 if core & 2 else core - 2


def routes(groups, count):
    last = count - 1
    ends = (0, 1, last - 1, last)

    def everywhere(pairs):
        return [(g * count + j, g * count + i) for g in range(groups) for j, i in pairs]

    def mirrored(step):
        sources = [i - step if i % 2 == 0 else i + step for i in range(count)]
        return [(j if 0 <= j <= last else i ^ 1, i) for i, j in enumerate(sources)]

    beside = everywhere([(i ^ 1, i) for i in range(count)])
    pair = everywhere([(i ^ 2, i) for i in range(count)])
    opposite = everywhere([((i + count // 2) % count ^ 1, i) for i in range(count)])
    third = everywhere(mirrored(4))
    across = everywhere([(i - 1 if i % 2 == 0 else i + 1, i) for i in range(count) if i not in (0, last)])
    side = everywhere([(i ^ 1 if i in ends else other_side(i), i) for i in range(count)])
    if groups > 1:
        across += [(g * count + i, (g + 1) % groups * count + i) for g in range(groups) for i in (0, last)]
    return beside, across, pair, side, third, opposite


def per_device(
    groups, vectors, near_index, near_block, basis, far_index, far_coupling, transfer, up_index, up_coupling
):
    leaves, rows, points = vectors.shape
    rank = basis.shape[2]
    packed = (leaves + 1) * rows // 2
    basis = jnp.swapaxes(basis, 1, 2)
    beside_to, across_to, pair_to, side_to, third_to, opposite_to = routes(groups, lax.axis_size("leaf"))

    def send(x, to):
        return lax.ppermute(x, ("groups", "leaf"), to)

    basis_beside = send(basis, beside_to)
    transfer_beside = send(transfer, beside_to)
    vectors_beside = send(vectors, beside_to)
    vectors_across = send(vectors, across_to)
    theirs, theirs_longer, theirs_longest, theirs_most = pl.pallas_call(
        coeffs_kernel,
        out_shape=tuple(jax.ShapeDtypeStruct((packed + extra, points), F32) for extra in (0, 8, 16, 24)),
        in_specs=[VMEM] * 3,
        out_specs=(VMEM,) * 4,
        compiler_params=room(4),
        cost_estimate=cost(5),
    )(vectors_beside, basis_beside, transfer_beside)
    pair = send(theirs, pair_to)
    side = send(theirs, side_to)
    opposite = send(theirs_longest, opposite_to)
    third = send(theirs_longer, third_to)
    own = send(theirs_most, beside_to)
    whole = jax.ShapeDtypeStruct(vectors.shape, F32)
    parts = jax.ShapeDtypeStruct((leaves, 2 * rank, points), jnp.bfloat16)
    high, low = pl.pallas_call(
        partner_matrices_kernel,
        out_shape=(parts, parts),
        in_specs=[VMEM] * 4,
        out_specs=(VMEM, VMEM),
        compiler_params=room(4),
        cost_estimate=cost(0),
    )(far_coupling, up_coupling, transfer, basis)
    vectors_across, side, pair, high, low = lax.optimization_barrier((vectors_across, side, pair, high, low))
    pair_beside = send(pair, beside_to)
    side_beside = send(side, beside_to)
    near = pl.pallas_call(
        near_kernel,
        out_shape=whole,
        in_specs=[VMEM] * 5,
        out_specs=VMEM,
        scratch_shapes=[pltpu.VMEM((3 * leaves, rows, points), F32)],
        compiler_params=room(8),
        cost_estimate=cost(0),
    )(near_index, near_block, vectors, vectors_beside, vectors_across)
    base = pl.pallas_call(
        far_kernel,
        out_shape=whole,
        in_specs=[VMEM] * 14,
        out_specs=VMEM,
        scratch_shapes=[pltpu.VMEM((7 * (leaves + 1), rows, points), F32)],
        compiler_params=room(10),
        cost_estimate=cost(0),
    )(
        far_index, up_index, near, own, theirs, pair_beside, pair, side_beside, side, third,
        far_coupling, up_coupling, transfer, basis,
    )
    return pl.pallas_call(
        partner_kernel,
        out_shape=whole,
        in_specs=[VMEM] * 4,
        out_specs=VMEM,
        compiler_params=room(4),
        cost_estimate=cost(0),
    )(base, opposite, high, low)


def solution(mesh):
    placed = (
        P(("groups", "leaf"), None, None),
        P(("groups", "leaf"), None),
        P(("groups", "leaf"), None, None, None),
        P(("groups", "leaf"), None, None),
        P(("groups", "leaf"), None),
        P(("groups", "leaf"), None, None, None),
        P(("groups", "leaf"), None, None),
        P(("groups", "leaf"), None),
        P(("groups", "leaf"), None, None, None),
    )
    return jax.shard_map(
        functools.partial(per_device, mesh.shape["groups"]),
        mesh=mesh,
        in_specs=placed,
        out_specs=P(("groups", "leaf"), None, None),
        check_vma=False,
    )
```
